32 devices in a mesh: dp: 4 (over y, x), seq: 8 (over z, core).
Axes of the slice: x: 2, y: 2, z: 4, core: 2. Of those that a mesh axis runs over, the one named last changes fastest.
Arguments:
- tokens: bfloat16 [8192, 1024], P(('dp', 'seq')), may hold values from -6 to 6
- lengths: int32 [4, 4], P('dp'), may hold values from 1 to 1793, 2048 in all within a row
- attn_gain: float32 [1024], replicated, may hold values from 0.5 to 1.5
- w_query: bfloat16 [1024, 1024], replicated, may hold values from -0.1875 to 0.1875
- w_key: bfloat16 [1024, 512], replicated, may hold values from -0.1875 to 0.1875
- w_value: bfloat16 [1024, 512], replicated, may hold values from -0.1875 to 0.1875
- query_gain: float32 [64], replicated, may hold values from 1 to 2
- key_gain: float32 [64], replicated, may hold values from 1 to 2
- w_out: bfloat16 [1024, 1024], replicated, may hold values from -0.75 to 0.75
- ffn_gain: float32 [1024], replicated, may hold values from 0.5 to 1.5
- w_gate: bfloat16 [1024, 4608], replicated, may hold values from -0.1875 to 0.1875
- w_up: bfloat16 [1024, 4608], replicated, may hold values from -0.1875 to 0.1875
- w_down: bfloat16 [4608, 1024], replicated, may hold values from -0.09375 to 0.09375
- cotangent: bfloat16 [8192, 1024], P(('dp', 'seq')), may hold values from -6 to 6
Outputs:
- mixed: bfloat16 [8192, 1024], P(('dp', 'seq'))
- grad_tokens: float32 [8192, 1024], P(('dp', 'seq'))
- grad_attn_gain: float32 [1024], replicated
- grad_w_query: float32 [1024, 1024], P(('dp', 'seq'))
- grad_w_key: float32 [1024, 512], P(('dp', 'seq'))
- grad_w_value: float32 [1024, 512], P(('dp', 'seq'))
- grad_query_gain: float32 [64], replicated
- grad_key_gain: float32 [64], replicated
- grad_w_out: float32 [1024, 1024], P(('dp', 'seq'))
- grad_ffn_gain: float32 [1024], replicated
- grad_w_gate: float32 [1024, 4608], P(('dp', 'seq'))
- grad_w_up: float32 [1024, 4608], P(('dp', 'seq'))
- grad_w_down: float32 [4608, 1024], P(('dp', 'seq'))
The draws below stay inside these ranges and needn't reach their ends.
Inputs may be any that keep to these rules, and one draw needn't show every extreme that they name: Each row holds the lengths of the 4 sequences packed in slot order into one data position's 2048 tokens; they sum to 2048 and the largest is exactly 1793.
All inputs are finite; a program needn't handle non-finite values.
Results may differ from the reference program's by a relative error of at most 0.015.
Values may be sent and summed in bfloat16 or wider, within the bound.
No kernel may reach another device: no remote copies, remote signals or barrier semaphores. Data moves between devices by JAX's collectives and lax.ppermute only.
A program may use at most 256 MiB of HBM per device.

```python
import math
import jax
import jax.numpy as jnp
import numpy as np
from jax import lax

D = 1024
FF = 4608
KVH = 8
HD = 64
QD = 1024
KVD = 512
GROUP_TOK = 2048
TOKENS = 8192
MOST = 1793
SLOTS = 4
N_DP = 4


def shard_levels(rng, shape, cuts, least, high):
    level = 1.0
    for axis_at, shards_of in cuts:
        steps = jax.random.uniform(jax.random.fold_in(jax.random.fold_in(rng, 6), axis_at), (shards_of,), jnp.float32, least / len(cuts), high / len(cuts))
        level = level * jnp.repeat(jnp.exp(steps), shape[axis_at] // shards_of).reshape((-1,) + (1,) * (len(shape) - 1 - axis_at))
    return level


def length_profile(amount, total, limit, slope):
    loads = [(1 << 20) // math.isqrt(grade ** slope) + 1 for grade in range(2, amount + 1)]
    spare, holding = total - limit - (amount - 1), [1] * (amount - 1)
    while spare > 0:
        free = [i for i in range(amount - 1) if holding[i] < limit]
        mass, remaining = sum([loads[i] for i in free]), spare
        for i in free:
            addition = min(limit - holding[i], max(1, remaining * loads[i] // mass), spare)
            holding[i] = holding[i] + addition
            spare = spare - addition
    return np.array([limit] + holding)


def uneven(stream_key, count, total, reach, slope):
    if count == 2:
        one = jax.random.randint(stream_key, (), max(1, total - reach), min(reach, total - 1) + 1)
        return jnp.stack([one, total - one])
    sizes = jnp.asarray(length_profile(count, total, reach, slope), jnp.int32)
    pairs = (count - 1) // 2
    giver, sink = sizes[1:1 + 2 * pairs:2], sizes[2:2 + 2 * pairs:2]
    slack = jnp.minimum(giver - 1, reach - sink)
    shifted = jax.random.randint(jax.random.fold_in(stream_key, 1), (pairs,), 0, 1 << 20) % (slack + 1)
    sizes = sizes.at[1:1 + 2 * pairs:2].set(giver - shifted).at[2:2 + 2 * pairs:2].set(sink + shifted)
    return sizes[jax.random.permutation(jax.random.fold_in(stream_key, 2), count)]


def scatter_about(rng, shape, scale, reach, cuts=(), held_as=jnp.bfloat16):
    level = shard_levels(rng, shape, cuts, -0.22, 0.18) if cuts else 1.0
    entries = jax.random.normal(rng, shape, jnp.float32) * scale * level
    return jnp.minimum(jnp.maximum(entries, -reach), reach).astype(held_as)


def setup_inputs(seed: int = 0) -> dict:
    splits = jax.random.split(jax.random.key(seed), 15)
    tokens = scatter_about(splits[0], (TOKENS, D), 1.0, 6.0, ((0, 32),))
    lengths = jax.vmap(lambda own: uneven(own, SLOTS, GROUP_TOK, MOST, 2))(jax.random.split(splits[1], N_DP)).reshape((N_DP, SLOTS)).astype(jnp.int32)
    attn_gain = jnp.clip(1.0 + 0.1 * jax.random.normal(splits[2], (D,), jnp.float32), 0.5, 1.5)
    w_query = scatter_about(splits[3], (D, QD), D ** -0.5, 0.1875)
    w_key = scatter_about(splits[4], (D, KVD), D ** -0.5, 0.1875)
    w_value = scatter_about(splits[5], (D, KVD), D ** -0.5, 0.1875)
    query_gain = jnp.clip(jax.random.uniform(splits[6], (HD,), jnp.float32, 1.0, 2.0), 1.0, 2.0)
    key_gain = jnp.clip(jax.random.uniform(splits[7], (HD,), jnp.float32, 1.0, 2.0), 1.0, 2.0)
    w_out = scatter_about(splits[8], (QD, D), (D // 16) ** -0.5, 0.75)
    ffn_gain = jnp.clip(1.0 + 0.1 * jax.random.normal(splits[9], (D,), jnp.float32), 0.5, 1.5)
    w_gate = scatter_about(splits[10], (D, FF), D ** -0.5, 0.1875)
    w_up = scatter_about(splits[11], (D, FF), D ** -0.5, 0.1875)
    w_down = scatter_about(splits[12], (FF, D), FF ** -0.5, 0.09375)
    cotangent = scatter_about(splits[13], (TOKENS, D), 1.0, 6.0, ((0, 32),))
    return dict(tokens=tokens, lengths=lengths, attn_gain=attn_gain, w_query=w_query, w_key=w_key, w_value=w_value, query_gain=query_gain, key_gain=key_gain, w_out=w_out, ffn_gain=ffn_gain, w_gate=w_gate, w_up=w_up, w_down=w_down, cotangent=cotangent)


EPSILON = 1e-05
ROPE_BASE = 1000000.0

@jax.custom_vjp
def low(v):
    return lax.optimization_barrier(v.astype(jnp.bfloat16)).astype(jnp.float32)

@jax.custom_vjp
def low_back(v):
    return v

def low_keep(v):
    return (low(v), None)

def low_pass(kept, grad):
    return (grad,)

def back_keep(v):
    return (v, None)

def back_low(kept, grad):
    return (low(grad),)
low.defvjp(low_keep, low_pass)
low_back.defvjp(back_keep, back_low)

def exact_dot(left, right):
    return jnp.dot(left, right, precision=lax.Precision.HIGHEST)

def rms_scale(field, gain_vec):
    return field * lax.rsqrt(lax.optimization_barrier(jnp.mean(field * field, axis=-1, keepdims=True)) + EPSILON) * gain_vec

def seg_info(tok_index, seq_lengths):
    seq_ends = jnp.cumsum(seq_lengths).astype(jnp.int32)
    seq_starts = (seq_ends - seq_lengths).astype(jnp.int32)
    inside = (tok_index[:, None] >= seq_starts[None, :]) & (tok_index[:, None] < seq_ends[None, :])
    slot_ids = jnp.arange(seq_lengths.shape[0], dtype=jnp.int32)
    segment = lax.optimization_barrier(jnp.sum(jnp.where(inside, slot_ids[None, :], 0), axis=1)).astype(jnp.int32)
    offset = lax.optimization_barrier(jnp.sum(jnp.where(inside, seq_starts[None, :], 0), axis=1)).astype(jnp.int32)
    return (segment, (tok_index - offset).astype(jnp.int32))

def rope_tables(position, head_size):
    half_size = head_size // 2
    freqs = ROPE_BASE ** (-2.0 * jnp.arange(half_size, dtype=jnp.float32) / head_size)
    angles = position.astype(jnp.float32)[:, None] * freqs[None, :]
    angles = jnp.concatenate([angles, angles], axis=1)
    return (jnp.cos(angles), jnp.sin(angles))

def rotate(field, cosine, sine):
    half_size = field.shape[-1] // 2
    turned = jnp.concatenate([-field[..., half_size:], field[..., :half_size]], axis=-1)
    return field * cosine[:, None, :] + turned * sine[:, None, :]

def normed_rotated(query_raw, key_raw, query_scale, key_scale, cosine, sine):
    head_size = query_scale.shape[0]
    tok_rows = query_raw.shape[0]
    queries = rms_scale(query_raw.reshape(tok_rows, -1, head_size), query_scale)
    key_rows = rms_scale(key_raw.reshape(tok_rows, -1, head_size), key_scale)
    return (rotate(queries, cosine, sine).reshape(tok_rows, -1), rotate(key_rows, cosine, sine).reshape(tok_rows, -1))

def kv_attend(queries, key_rows, value_rows, keep_mask):
    score_scale = queries.shape[-1] ** (-0.5)
    raw_scores = jnp.einsum('qrd,kd->rqk', queries, key_rows, precision=lax.Precision.HIGHEST) * score_scale
    scores = low_back(raw_scores)
    masked = jnp.where(keep_mask[None], scores, -1e+30)
    row_max = lax.optimization_barrier(jnp.max(masked, axis=-1, keepdims=True))
    exp_terms = jnp.exp(masked - row_max)
    weights = low(exp_terms / lax.optimization_barrier(jnp.sum(exp_terms, axis=-1, keepdims=True)))
    return jnp.einsum('rqk,kd->qrd', weights, value_rows, precision=lax.Precision.HIGHEST)

def reference(tokens, lengths, attn_gain, w_query, w_key, w_value, query_gain, key_gain, w_out, ffn_gain, w_gate, w_up, w_down, cotangent):
    tok_total = tokens.shape[0]
    groups = lengths.shape[0]
    group_rows = tok_total // groups
    tok_index = jnp.arange(group_rows, dtype=jnp.int32)
    position = jax.vmap(lambda seq_lengths: seg_info(tok_index, seq_lengths)[1])(lengths).reshape(tok_total)
    cosine, sine = rope_tables(position, HD)

    def forward(inputs, a_gain, wq_full, wk_full, wv_full, q_gain, k_gain, wo_full, f_gain, wg_full, wu_full, wd_full):
        normed = low(rms_scale(inputs, a_gain))
        query_raw = low_back(exact_dot(normed, wq_full))
        key_raw = low_back(exact_dot(normed, wk_full))
        values = low_back(low(exact_dot(normed, wv_full)))
        query_turned, key_turned = normed_rotated(query_raw, key_raw, q_gain, k_gain, cosine, sine)
        queries = low_back(low(query_turned))
        key_rows = low_back(low(key_turned))
        query_groups = queries.reshape(groups, group_rows, KVH, 2, HD)
        key_groups = key_rows.reshape(groups, group_rows, KVH, HD)
        value_groups = values.reshape(groups, group_rows, KVH, HD)

        def one_group(items):
            group_q, group_k, group_v, seq_lengths = items
            segment, unused_pos = seg_info(tok_index, seq_lengths)
            keep_mask = (segment[:, None] == segment[None, :]) & (tok_index[None, :] <= tok_index[:, None])

            def one_head(pieces):
                return kv_attend(pieces[0], pieces[1], pieces[2], keep_mask)
            per_head = lax.map(jax.checkpoint(one_head), (jnp.moveaxis(group_q, 1, 0), jnp.moveaxis(group_k, 1, 0), jnp.moveaxis(group_v, 1, 0)))
            return jnp.moveaxis(per_head, 0, 1)
        attended = lax.map(one_group, (query_groups, key_groups, value_groups, lengths))
        heads_out = low_back(low(attended.reshape(tok_total, QD)))
        middle = inputs + low_back(exact_dot(heads_out, wo_full))
        normed_two = low(rms_scale(middle, f_gain))
        gate = low_back(exact_dot(normed_two, wg_full))
        up_proj = low_back(exact_dot(normed_two, wu_full))
        activated = low(jax.nn.silu(gate) * up_proj)
        return middle + low_back(exact_dot(activated, wd_full))
    params = (tokens.astype(jnp.float32), attn_gain, w_query.astype(jnp.float32), w_key.astype(jnp.float32), w_value.astype(jnp.float32), query_gain, key_gain, w_out.astype(jnp.float32), ffn_gain, w_gate.astype(jnp.float32), w_up.astype(jnp.float32), w_down.astype(jnp.float32))
    output, pull = jax.vjp(forward, *params)
    grads = pull(cotangent.astype(jnp.float32))
    return (output.astype(jnp.bfloat16), grads[0], grads[1], grads[2], grads[3], grads[4], grads[5], grads[6], grads[7], grads[8], grads[9], grads[10], grads[11])
```

```python
import functools
import math

import jax
import jax.numpy as jnp
from jax import lax
from jax.experimental import pallas as pl
from jax.experimental.pallas import tpu as pltpu
from jax.sharding import Mesh
from jax.sharding import PartitionSpec as P

EPSILON = 1e-05
ROPE_BASE = 1000000.0
FAR = 16384.0
LANES = 128
VMEM_LIMIT = 56 * 1024 * 1024
ALL = ("y", "x", "z", "c")
F32 = jnp.float32
BF16 = jnp.bfloat16


def dot_nn(left, right):
    return lax.dot_general(left, right, (((1,), (0,)), ((), ())), preferred_element_type=F32)


def dot_nt(left, right):
    return lax.dot_general(left, right, (((1,), (1,)), ((), ())), preferred_element_type=F32)


def dot_tn(left, right):
    return lax.dot_general(left, right, (((0,), (0,)), ((), ())), preferred_element_type=F32)


def params():
    return pltpu.CompilerParams(vmem_limit_bytes=VMEM_LIMIT)


def pick(field, index, axis=0):
    return lax.dynamic_index_in_dim(field, index, axis, keepdims=False)


def swap(field, axis_name):
    return lax.ppermute(field, axis_name, [(0, 1), (1, 0)])


def both(own, other, core):
    rows = own.shape[0]
    first = jnp.where(core == 0, own, other)
    second = jnp.where(core == 0, other, own)
    return jnp.concatenate([first, second], axis=0)


def pair_reduce(parts, axis_name, index):
    got = swap(pick(parts, 1 - index), axis_name)
    return pick(parts, index) + got


def line_reduce(parts, axis_name, index):
    count = parts.shape[0]

    def part(number):
        return pick(parts, jnp.clip(number, 0, count - 1))

    right = left = None
    for step in range(1, count):
        to_right = part(count - step + index)
        to_left = part(step - count + index)
        if right is not None:
            to_right = to_right + right
            to_left = to_left + left
        right = lax.ppermute(to_right, axis_name, [(k, k + 1) for k in range(step)])
        left = lax.ppermute(
            to_left, axis_name, [(count - 1 - k, count - 2 - k) for k in range(step)]
        )
    return part(index) + right + left


def reduce_first(parts, axis_name, index):
    if parts.shape[0] == 1:
        return parts[0]
    if axis_name == "z":
        return line_reduce(parts, axis_name, index)
    if parts.shape[0] == 2:
        return pair_reduce(parts, axis_name, index)
    return lax.psum_scatter(parts, axis_name, scatter_dimension=0, tiled=False)


def exchange_line(parts, index):
    count = parts.shape[0]
    got = []
    for step in range(count - 1, 0, -1):
        arrived = lax.ppermute(
            pick(parts, index ^ step), "z", [(k, k ^ step) for k in range(count)]
        )
        got.append((index ^ step, arrived))
    out = lax.dynamic_update_index_in_dim(jnp.zeros_like(parts), pick(parts, index), index, 0)
    for place, arrived in got:
        out = lax.dynamic_update_index_in_dim(out, arrived, place, 0)
    return out


def sum_all(vector, rows_y, rows_z):
    vector = vector + swap(vector, "c")
    vector = vector + swap(vector, "x")
    if rows_y == 2:
        vector = vector + swap(vector, "y")
    else:
        vector = lax.psum(vector, "y")
    step = 1
    while step < rows_z:
        vector = vector + lax.ppermute(vector, "z", [(k, k ^ step) for k in range(rows_z)])
        step = step * 2
    return vector


def lane_ids(rows):
    return lax.broadcasted_iota(jnp.int32, (rows, LANES), 1)


def half_swap(field, lanes):
    return jnp.where(
        (lanes & 63) < 32, pltpu.roll(field, LANES - 32, 1), pltpu.roll(field, 32, 1)
    )


def half_sums(field, lanes):
    low = jnp.sum(jnp.where(lanes < 64, field, 0.0), axis=1, keepdims=True)
    high = jnp.sum(jnp.where(lanes < 64, 0.0, field), axis=1, keepdims=True)
    return jnp.where(lanes < 64, low, high)


def project_kernel(head_size, ids, x_ref, gain_ref, wq_ref, wk_ref, wv_ref, cos_ref, sin_ref,
                   qg_ref, kg_ref, h_ref, out_ref):
    rows = x_ref.shape[0]
    x = x_ref[...].astype(F32)
    scale = lax.rsqrt(jnp.mean(x * x, axis=1, keepdims=True) + EPSILON)
    h = (x * scale * gain_ref[...]).astype(BF16)
    h_ref[...] = h
    lanes = lane_ids(rows)
    cosine, sine = cos_ref[...], sin_ref[...]

    def turned(raw, gain):
        unit = raw * lax.rsqrt(half_sums(raw * raw, lanes) * (1.0 / head_size) + EPSILON) * gain
        return unit * cosine + half_swap(unit, lanes) * sine

    q_raw = dot_nn(h, wq_ref[...])
    k_raw = dot_nn(h, wk_ref[...])
    v_raw = dot_nn(h, wv_ref[...])
    heads = out_ref.shape[0]
    for head in range(heads):
        span = slice(head * LANES, (head + 1) * LANES)
        out_ref[head, :, 0:LANES] = turned(q_raw[:, span], qg_ref[...]).astype(BF16)
    for pair in range(heads // 2):
        span = slice(pair * LANES, (pair + 1) * LANES)
        keys = turned(k_raw[:, span], kg_ref[...])
        values = v_raw[:, span]
        even = jnp.where(lanes < 64, keys, pltpu.roll(values, 64, 1))
        odd = jnp.where(lanes < 64, pltpu.roll(keys, 64, 1), values)
        out_ref[2 * pair, :, LANES:] = even.astype(BF16)
        out_ref[2 * pair + 1, :, LANES:] = odd.astype(BF16)


def project(ids, x, gain, w_query, w_key, w_value, cosine, sine, qg, kg, head_size):
    rows, width = x.shape
    heads = w_key.shape[1] // head_size // 2
    block = min(256, rows)
    whole = lambda shape: pl.BlockSpec(shape, lambda i, ids: (0,) * len(shape))
    by_core = lambda w: pl.BlockSpec((width, w.shape[1] // 2), lambda i, ids: (0, ids[0]))
    by_row = lambda cols: pl.BlockSpec((block, cols), lambda i, ids: (i, 0))
    return pl.pallas_call(
        functools.partial(project_kernel, head_size),
        grid_spec=pltpu.PrefetchScalarGridSpec(
            num_scalar_prefetch=1,
            grid=(rows // block,),
            in_specs=[by_row(width), whole((1, width)), by_core(w_query), by_core(w_key),
                      by_core(w_value), by_row(LANES), by_row(LANES), whole((1, LANES)),
                      whole((1, LANES))],
            out_specs=[by_row(width),
                       pl.BlockSpec((heads, block, 2 * LANES), lambda i, ids: (0, i, 0))],
        ),
        out_shape=[jax.ShapeDtypeStruct((rows, width), BF16),
                   jax.ShapeDtypeStruct((heads, rows, 2 * LANES), BF16)],
        compiler_params=params(),
        cost_estimate=pl.CostEstimate(
            flops=2 * rows * width * w_query.shape[1], bytes_accessed=6 << 20, transcendentals=0),
        name="project",
    )(ids, x, gain, w_query, w_key, w_value, cosine, sine, qg, kg)


def three_parts(value):
    high = value.astype(BF16).astype(F32)
    rest = value - high
    middle = rest.astype(BF16).astype(F32)
    return high, middle, rest - middle


def marked(lanes, first, value, otherwise):
    high, middle, low = three_parts(value)
    return jnp.where(
        lanes == first,
        high,
        jnp.where(lanes == first + 1, middle, jnp.where(lanes == first + 2, low, otherwise)),
    )


def below(rows, cols):
    return lax.broadcasted_iota(jnp.int32, (rows, cols), 1) <= lax.broadcasted_iota(
        jnp.int32, (rows, cols), 0
    )


def attend_kernel(block, mark, qkv_ref, segq_ref, segk_ref, o_ref, wide_ref, qaug_ref, kaug_ref,
                  vaug_ref):
    rows = qkv_ref.shape[0]
    count = rows // block
    lanes = lane_ids(block)
    for i in range(count):
        span = slice(i * block, (i + 1) * block)
        pair = qkv_ref[span, 0:LANES].astype(F32)
        keyval = qkv_ref[span, LANES:].astype(F32)
        segq = segq_ref[span, :].astype(F32)
        segk = segk_ref[span, :].astype(F32)
        qaug_ref[0, span, :] = jnp.where(lanes < 64, pair, segq).astype(BF16)
        qaug_ref[1, span, :] = jnp.where(lanes < 64, pltpu.roll(pair, 64, 1), segq).astype(BF16)
        kaug_ref[span, :] = jnp.where(lanes < 64, keyval, segk).astype(BF16)
        vaug_ref[span, :] = jnp.where(
            lanes < 64, pltpu.roll(keyval, 64, 1), jnp.where(lanes < 67, 1.0, 0.0)
        ).astype(BF16)
    for i in range(count):
        span = slice(i * block, (i + 1) * block)
        outs = []
        for head in range(2):
            queries = qaug_ref[head, span, :]
            total = jnp.zeros((block, LANES), F32)
            for j in range(i + 1):
                other = slice(j * block, (j + 1) * block)
                weights = jnp.exp2(dot_nt(queries, kaug_ref[other, :]))
                if j == i:
                    weights = jnp.where(below(block, block), weights, 0.0)
                total = total + dot_nn(weights.astype(BF16), vaug_ref[other, :])
            row_sum = total[:, 64:65]
            outs.append(total * (1.0 / row_sum))
            qaug_ref[head, span, :] = marked(
                lanes, mark, -jnp.log2(row_sum), queries.astype(F32)
            ).astype(BF16)
        wide = jnp.where(lanes < 64, outs[0], pltpu.roll(outs[1], 64, 1))
        wide_ref[span, :] = wide
        o_ref[span, :] = wide.astype(BF16)


def attend(qkv, segq, segk, block, mark):
    rows = qkv.shape[0]
    return pl.pallas_call(
        functools.partial(attend_kernel, block, mark),
        out_shape=[jax.ShapeDtypeStruct((rows, LANES), BF16),
                   jax.ShapeDtypeStruct((rows, LANES), F32),
                   jax.ShapeDtypeStruct((2, rows, LANES), BF16),
                   jax.ShapeDtypeStruct((rows, LANES), BF16),
                   jax.ShapeDtypeStruct((rows, LANES), BF16)],
        compiler_params=params(),
        cost_estimate=pl.CostEstimate(
            flops=rows * rows * LANES * 8, bytes_accessed=6 << 20,
            transcendentals=rows * rows),
        name="attend",
    )(qkv, segq, segk)


def attend_back_kernel(block, qaug_ref, kaug_ref, vaug_ref, wide_ref, do_ref, dq_ref, dkv_ref,
                       doaug, dq_sum):
    rows = kaug_ref.shape[0]
    count = rows // block
    lanes = lane_ids(block)
    for i in range(count):
        span = slice(i * block, (i + 1) * block)
        do_pair = do_ref[span, :].astype(F32)
        inner = do_pair * wide_ref[span, :]
        low = jnp.sum(jnp.where(lanes < 64, inner, 0.0), axis=1, keepdims=True)
        high = jnp.sum(jnp.where(lanes < 64, 0.0, inner), axis=1, keepdims=True)
        doaug[0, span, :] = jnp.where(
            lanes < 64, do_pair, marked(lanes, 64, -low, 0.0)).astype(BF16)
        doaug[1, span, :] = jnp.where(
            lanes < 64, pltpu.roll(do_pair, 64, 1), marked(lanes, 64, -high, 0.0)).astype(BF16)
        dq_sum[:, span, :] = jnp.zeros((2, block, LANES), F32)
    for j in range(count):
        here = slice(j * block, (j + 1) * block)
        keys = kaug_ref[here, :]
        values = vaug_ref[here, :]
        dk = jnp.zeros((LANES, block), F32)
        dv = jnp.zeros((LANES, block), F32)
        for i in range(j, count):
            span = slice(i * block, (i + 1) * block)
            for head in range(2):
                queries = qaug_ref[head, span, :]
                grads = doaug[head, span, :]
                weights = jnp.exp2(dot_nt(queries, keys))
                if j == i:
                    weights = jnp.where(below(block, block), weights, 0.0)
                slopes = (weights * dot_nt(grads, values)).astype(BF16)
                dv = dv + dot_tn(grads, weights.astype(BF16))
                dk = dk + dot_tn(queries, slopes)
                dq_sum[head, span, :] = dq_sum[head, span, :] + dot_nn(slopes, keys)
        dk_rows = jnp.transpose(dk) * math.log(2.0)
        dv_rows = jnp.transpose(dv)
        dkv_ref[here, :] = jnp.where(lanes < 64, dk_rows, pltpu.roll(dv_rows, 64, 1))
    for i in range(count):
        span = slice(i * block, (i + 1) * block)
        dq_ref[span, :] = jnp.where(
            lanes < 64, dq_sum[0, span, :], pltpu.roll(dq_sum[1, span, :], 64, 1)) * 0.125


def attend_back(qaug, kaug, vaug, wide, do, block):
    rows = kaug.shape[0]
    return pl.pallas_call(
        functools.partial(attend_back_kernel, block),
        out_shape=[jax.ShapeDtypeStruct((rows, LANES), F32)] * 2,
        scratch_shapes=[pltpu.VMEM((2, rows, LANES), BF16), pltpu.VMEM((2, rows, LANES), F32)],
        compiler_params=params(),
        cost_estimate=pl.CostEstimate(
            flops=rows * rows * LANES * 20, bytes_accessed=6 << 20,
            transcendentals=rows * rows),
        name="attend_back",
    )(qaug, kaug, vaug, wide, do)


def unturn_kernel(head_size, ids, h_ref, wq_ref, wk_ref, cos_ref, sin_ref, qg_ref, kg_ref, dq_ref,
                  dkv_ref, out_ref, gains_ref):
    rows = h_ref.shape[0]
    lanes = lane_ids(rows)
    cosine, sine = cos_ref[...], sin_ref[...]
    h = h_ref[...]

    def undo(raw, grad, gain):
        scale = lax.rsqrt(half_sums(raw * raw, lanes) * (1.0 / head_size) + EPSILON)
        unit = raw * scale
        back = grad * cosine - half_swap(grad, lanes) * sine
        scaled = back * gain
        mean = half_sums(scaled * unit, lanes) * (1.0 / head_size)
        return scale * (scaled - unit * mean), jnp.sum(back * unit, axis=0, keepdims=True)

    q_raw = dot_nn(h, wq_ref[...])
    k_pair = dot_nn(h, wk_ref[...])
    k_raw = jnp.where(ids[2] == 0, k_pair, pltpu.roll(k_pair, 64, 1))
    dkv = dkv_ref[...]
    dqr, q_gain = undo(q_raw, dq_ref[...], qg_ref[...])
    dkr, k_gain = undo(k_raw, jnp.where(lanes < 64, dkv, 0.0), kg_ref[...])
    out_ref[:, 0:LANES] = dqr.astype(BF16)
    out_ref[:, LANES:] = jnp.where(lanes < 64, dkr, dkv).astype(BF16)

    @pl.when(pl.program_id(0) == 0)
    def _():
        gains_ref[...] = jnp.zeros_like(gains_ref)

    gains_ref[0:1, :] = gains_ref[0:1, :] + q_gain
    gains_ref[1:2, :] = gains_ref[1:2, :] + k_gain


def unturn(ids, h, w_query, w_key, cosine, sine, qg, kg, dq, dkv, head_size):
    rows, width = h.shape
    block = min(512, rows)
    whole = lambda shape: pl.BlockSpec(shape, lambda i, ids: (0,) * len(shape))
    by_row = lambda cols: pl.BlockSpec((block, cols), lambda i, ids: (i, 0))
    return pl.pallas_call(
        functools.partial(unturn_kernel, head_size),
        grid_spec=pltpu.PrefetchScalarGridSpec(
            num_scalar_prefetch=1,
            grid=(rows // block,),
            in_specs=[by_row(width),
                      pl.BlockSpec((width, LANES), lambda i, ids: (0, ids[1])),
                      pl.BlockSpec((width, LANES), lambda i, ids: (0, ids[1] // 2)),
                      by_row(LANES), by_row(LANES), whole((1, LANES)), whole((1, LANES)),
                      by_row(LANES), by_row(LANES)],
            out_specs=[by_row(2 * LANES), whole((8, LANES))],
        ),
        out_shape=[jax.ShapeDtypeStruct((rows, 2 * LANES), BF16),
                   jax.ShapeDtypeStruct((8, LANES), F32)],
        compiler_params=params(),
        cost_estimate=pl.CostEstimate(
            flops=4 * rows * width * LANES, bytes_accessed=10 << 20, transcendentals=0),
        name="unturn",
    )(ids, h, w_query, w_key, cosine, sine, qg, kg, dq, dkv)


def feed_kernel(ids, h_ref, c_ref, wg_ref, wu_ref, wd_ref, *refs):
    m_ref, dg_ref, du_ref, dh_ref, y_ref = refs[-5:]
    h, c = h_ref[...], c_ref[...]
    gate = dot_nn(h, wg_ref[...])
    up = dot_nn(h, wu_ref[...])
    sig = jax.nn.sigmoid(gate)
    silu = gate * sig
    m = (silu * up).astype(BF16)
    m_ref[...] = m
    y_ref[...] = dot_nn(m, wd_ref[...]).astype(BF16)
    dm = dot_nt(c, wd_ref[...])
    dg = (dm * up * sig * (1.0 + gate * (1.0 - sig))).astype(BF16)
    du = (dm * silu).astype(BF16)
    dg_ref[...] = dg
    du_ref[...] = du
    dh_ref[...] = (dot_nt(dg, wg_ref[...]) + dot_nt(du, wu_ref[...])).astype(BF16)


def feed(ids, h, c, w_gate, w_up, w_down, earlier, parts):
    rows, width = h.shape
    units = w_gate.shape[1] // parts
    block = min(256, rows)
    steps = rows // block
    half = 0 if earlier is None else 1
    by_row = pl.BlockSpec((block, width), lambda i, ids: (i, 0))
    in_cols = pl.BlockSpec((width, units), lambda i, ids: (0, ids[3]))
    kept = pl.BlockSpec((block, units), lambda i, ids: (i + half * steps, 0))
    extra = () if earlier is None else tuple(earlier)
    big = jax.ShapeDtypeStruct((2 * rows, units), BF16)
    small = jax.ShapeDtypeStruct((rows, width), BF16)
    return pl.pallas_call(
        feed_kernel,
        grid_spec=pltpu.PrefetchScalarGridSpec(
            num_scalar_prefetch=1,
            grid=(steps,),
            in_specs=[by_row, by_row, in_cols, in_cols,
                      pl.BlockSpec((units, width), lambda i, ids: (ids[3], 0))]
            + [pl.BlockSpec(memory_space=pl.ANY)] * len(extra),
            out_specs=[kept, kept, kept, by_row, by_row],
        ),
        out_shape=[big, big, big, small, small],
        input_output_aliases={6 + k: k for k in range(len(extra))},
        compiler_params=params(),
        cost_estimate=pl.CostEstimate(
            flops=12 * rows * width * units, bytes_accessed=16 << 20,
            transcendentals=rows * units),
        name="feed",
    )(ids, h, c, w_gate, w_up, w_down, *extra)


def norm_scale(field):
    return lax.rsqrt(jnp.mean(field * field, axis=-1, keepdims=True) + EPSILON)


def norm_back(field, scale, scaled_grad):
    inner = jnp.mean(scaled_grad * field, axis=-1, keepdims=True)
    return scale * scaled_grad - field * (scale * scale * scale * inner)


def rope_tables(position, head_size):
    half = head_size // 2
    lane = jnp.arange(LANES, dtype=jnp.int32)
    freqs = ROPE_BASE ** (-2.0 * (lane % half).astype(F32) / head_size)
    angles = position.astype(F32)[:, None] * freqs[None, :]
    sign = jnp.where(lane % head_size < half, -1.0, 1.0)
    return jnp.cos(angles), jnp.sin(angles) * sign[None, :]


def body(tokens, lengths, attn_gain, w_query, w_key, w_value, query_gain, key_gain, w_out,
         ffn_gain, w_gate, w_up, w_down, cotangent):
    rows, width = tokens.shape
    head_size = query_gain.shape[0]
    n_y, n_z = lax.axis_size("y"), lax.axis_size("z")
    i_y, i_x, i_z, i_c = (lax.axis_index(name) for name in ALL)
    chip_rows = 2 * rows
    group_rows = chip_rows * n_z
    kv_heads = w_key.shape[1] // head_size
    heads = kv_heads // 2
    slots = lengths.shape[1]
    mark = 64 + slots
    head = i_c * heads + i_z
    ids = jnp.stack([i_c, head, head % 2, 2 * i_x + i_c]).astype(jnp.int32)

    x = both(tokens, swap(tokens, "c"), i_c)
    cot = both(cotangent, swap(cotangent, "c"), i_c)
    cot_far_own = swap(cotangent, "x")
    cot_far = both(cot_far_own, swap(cot_far_own, "c"), i_c)

    index = jnp.arange(group_rows, dtype=jnp.int32)
    lane = jnp.arange(LANES, dtype=jnp.int32)
    start_of = jnp.zeros((group_rows,), jnp.int32)
    lane_start = jnp.zeros((LANES,), jnp.int32)
    lane_end = jnp.zeros((LANES,), jnp.int32)
    run = jnp.zeros((), jnp.int32)
    for slot in range(slots):
        stop = run + lengths[0, slot]
        start_of = jnp.where((index >= run) & (index < stop), run, start_of)
        lane_start = jnp.where(lane == 64 + slot, run, lane_start)
        lane_end = jnp.where(lane == 64 + slot, stop, lane_end)
        run = stop
    inside = (index[:, None] >= lane_start[None, :]) & (index[:, None] < lane_end[None, :])
    slot_lane = (lane >= 64) & (lane < mark)
    ones_lane = (lane >= mark) & (lane < mark + 3)
    segq = jnp.where(inside, 1.0, 0.0).astype(BF16)
    segk = jnp.where(
        slot_lane[None, :], jnp.where(inside, 0.0, -FAR), jnp.where(ones_lane, 1.0, 0.0)[None, :]
    ).astype(BF16)
    position = index - start_of
    cos_all, sin_all = rope_tables(position, head_size)
    cosine = lax.dynamic_slice_in_dim(cos_all, i_z * chip_rows, chip_rows, 0)
    sine = lax.dynamic_slice_in_dim(sin_all, i_z * chip_rows, chip_rows, 0)

    to_exp2 = math.log2(math.e) / math.sqrt(head_size)
    qg = jnp.tile(query_gain, 2)[None, :]
    kg = jnp.tile(key_gain, 2)[None, :]
    h, packed = project(ids, x, attn_gain[None, :], w_query, w_key, w_value, cosine, sine,
                        qg * to_exp2, kg, head_size)
    qkv = exchange_line(packed, i_z).reshape(group_rows, 2 * LANES)
    block = math.gcd(512, group_rows)
    o_head, wide, qaug, kaug, vaug = attend(qkv, segq, segk, block, mark)
    o_own = exchange_line(o_head.reshape(n_z, chip_rows, LANES), i_z)
    o_other = swap(o_own, "c")
    o_first = jnp.where(i_c == 0, o_own, o_other)
    o_second = jnp.where(i_c == 0, o_other, o_own)
    o_all = jnp.concatenate([o_first, o_second], axis=0)
    o_rows = jnp.transpose(o_all, (1, 0, 2)).reshape(chip_rows, width)
    middle = x.astype(F32) + dot_nn(o_rows, w_out)
    scale_two = norm_scale(middle)
    h2 = (middle * scale_two * ffn_gain[None, :]).astype(BF16)

    h2_own = lax.dynamic_slice_in_dim(h2, i_c * rows, rows, 0)
    far_own = swap(h2_own, "x")
    h2_far = both(far_own, swap(far_own, "c"), i_c)
    m, dg, du, dh2_near, y_near = feed(ids, h2, cot, w_gate, w_up, w_down, None, 4)
    m, dg, du, dh2_far, y_far = feed(ids, h2_far, cot_far, w_gate, w_up, w_down, (m, dg, du), 4)

    def home(near, far):
        far_sum = pair_reduce(far.reshape(2, rows, width), "c", i_c)
        near_sum = pair_reduce(near.reshape(2, rows, width), "c", i_c)
        return near_sum.astype(F32) + swap(far_sum, "x").astype(F32)

    dh2 = home(dh2_near, dh2_far)
    own = lambda field: lax.dynamic_slice_in_dim(field, i_c * rows, rows, 0)
    middle_own, scale_own = own(middle), own(scale_two)
    dy = cotangent.astype(F32) + norm_back(middle_own, scale_own, dh2 * ffn_gain[None, :])
    gain_ffn = jnp.sum(dh2 * middle_own * scale_own, axis=0)
    da_own = dy.astype(BF16)
    da = both(da_own, swap(da_own, "c"), i_c)
    w_out_own = lax.dynamic_slice_in_dim(w_out, i_c * (width // 2), width // 2, 0)
    do = dot_nt(da, w_out_own).astype(BF16)
    do_parts = jnp.transpose(do.reshape(chip_rows, heads, LANES), (1, 0, 2))
    do_head = exchange_line(do_parts, i_z).reshape(group_rows, LANES)

    mixed = (middle_own + home(y_near, y_far)).astype(BF16)

    h2_all = jnp.concatenate([h2, h2_far], axis=0)
    cot_all = jnp.concatenate([cot, cot_far], axis=0)
    units = m.shape[1]
    piece = units // (n_y * n_z)
    down = dot_tn(m, cot_all).astype(BF16).reshape(n_z, n_y, piece, width)
    down = reduce_first(jnp.moveaxis(down, 1, 0), "y", i_y)
    down = line_reduce(down, "z", i_z)
    owners = []
    for y in range(n_y):
        for xx in range(2):
            for z in range(n_z):
                for c in range(2):
                    source = ((y * 2 + xx) * n_z + z) * 2 + c
                    owners.append((source, 4 * 0 + n_y * n_z * (2 * xx + c) + z * n_y + y))
    share_down = lax.ppermute(down, ALL, owners).astype(F32)

    row_block = width // (n_y * 2 * n_z * 2)

    def rows_home(grad):
        cols = grad.shape[1]
        parts = grad.reshape(n_y, 2, n_z, 2, row_block, cols)
        parts = reduce_first(parts, "y", i_y)
        parts = line_reduce(jnp.moveaxis(parts, 1, 0), "z", i_z)
        return parts

    def spread(parts):
        kept = pick(parts, i_c, 1)
        got = swap(pick(parts, 1 - i_c, 1), "c")
        cols = jnp.concatenate(
            [jnp.where(i_c == 0, kept, got), jnp.where(i_c == 0, got, kept)], axis=2)
        kept = pick(cols, i_x)
        got = swap(pick(cols, 1 - i_x), "x")
        return jnp.concatenate(
            [jnp.where(i_x == 0, kept, got), jnp.where(i_x == 0, got, kept)], axis=1).astype(F32)

    share_gate = spread(rows_home(dot_tn(h2_all, dg).astype(BF16)))
    share_up = spread(rows_home(dot_tn(h2_all, du).astype(BF16)))

    da_cols = lax.dynamic_slice_in_dim(da, i_c * (width // 2), width // 2, 1)
    out_parts = dot_tn(o_rows, da_cols).astype(BF16).reshape(
        n_y, 2, n_z, 2, row_block, width // 2)
    out_parts = pair_reduce(jnp.moveaxis(out_parts, 1, 0), "x", i_x)
    out_parts = reduce_first(out_parts, "y", i_y)
    out_parts = line_reduce(out_parts, "z", i_z)
    kept = pick(out_parts, i_c)
    got = swap(pick(out_parts, 1 - i_c), "c")
    share_out = jnp.concatenate(
        [jnp.where(i_c == 0, kept, got), jnp.where(i_c == 0, got, kept)], axis=1).astype(F32)

    h_own = own(h)
    blocks = jnp.zeros((n_z, chip_rows, width), BF16)
    blocks = lax.dynamic_update_index_in_dim(blocks, h, i_z, 0)
    right = left = h_own
    for step in range(1, n_z):
        right = lax.ppermute(right, "z", [(k, k + 1) for k in range(n_z - 1)])
        left = lax.ppermute(left, "z", [(k + 1, k) for k in range(n_z - 1)])
        for sent, place in ((right, i_z - step), (left, i_z + step)):
            full = both(sent, swap(sent, "c"), i_c)
            inside_line = (place >= 0) & (place < n_z)
            spot = jnp.clip(place, 0, n_z - 1)
            full = jnp.where(inside_line, full, pick(blocks, spot))
            blocks = lax.dynamic_update_index_in_dim(blocks, full, spot, 0)
    h_group = blocks.reshape(group_rows, width)

    dq, dkv = attend_back(qaug, kaug, vaug, wide, do_head, block)
    back, gains = unturn(ids, h_group, w_query, w_key, cos_all, sin_all, qg, kg, dq, dkv, head_size)
    back_own = exchange_line(back.reshape(n_z, chip_rows, 2 * LANES), i_z)

    half = lambda w, cols: lax.dynamic_slice_in_dim(
        w, i_c * heads * cols, heads * cols, 1).reshape(width, heads, cols)
    w_heads = jnp.concatenate(
        [half(w_query, LANES), half(w_key, head_size), half(w_value, head_size)], axis=2)
    dh_part = lax.dot_general(
        back_own, w_heads, (((0, 2), (1, 2)), ((), ())), preferred_element_type=F32)
    dh = pair_reduce(dh_part.astype(BF16).reshape(2, rows, width), "c", i_c).astype(F32)

    grad_head = dot_tn(h_group, back)
    gain_attn = jnp.sum(grad_head * pick(w_heads, i_z, 1).astype(F32), axis=1) / attn_gain
    parts = grad_head.astype(BF16).reshape(n_y, 2, n_z, 2, row_block, 2 * LANES)
    parts = pair_reduce(jnp.moveaxis(parts, 1, 0), "x", i_x)
    parts = reduce_first(parts, "y", i_y)
    parts = exchange_line(parts, i_z)
    kept = pick(parts, i_c, 1)
    got = swap(pick(parts, 1 - i_c, 1), "c")
    by_head = jnp.concatenate(
        [jnp.where(i_c == 0, kept, got), jnp.where(i_c == 0, got, kept)], axis=0)
    by_head = jnp.transpose(by_head, (1, 0, 2)).astype(F32)
    share_query = by_head[:, :, :LANES].reshape(row_block, -1)
    share_key = by_head[:, :, LANES : LANES + head_size].reshape(row_block, -1)
    share_value = by_head[:, :, LANES + head_size :].reshape(row_block, -1)

    x_own = tokens.astype(F32)
    grad_tokens = dy + norm_back(x_own, norm_scale(x_own), dh * attn_gain[None, :])

    gain_query = gains[0, :head_size] + gains[0, head_size:]
    gain_key = gains[1, :head_size]
    sums = sum_all(
        jnp.concatenate([gain_attn, gain_ffn, gain_query, gain_key]).reshape(1, -1), n_y, n_z)[0]
    return (
        mixed,
        grad_tokens,
        sums[:width],
        share_query,
        share_key,
        share_value,
        sums[2 * width : 2 * width + head_size],
        sums[2 * width + head_size :],
        share_out,
        sums[width : 2 * width],
        share_gate,
        share_up,
        share_down,
    )


def solution(mesh):
    n_dp, n_seq = mesh.shape["dp"], mesh.shape["seq"]
    fine = Mesh(mesh.devices.reshape(n_dp // 2, 2, n_seq // 2, 2), ALL)
    split = P(ALL, None)
    in_specs = (split, P(("y", "x"), None)) + (P(),) * 11 + (split,)
    out_specs = (split, split, P(), split, split, split, P(), P(), split, P(), split, split, split)
    return jax.shard_map(body, mesh=fine, in_specs=in_specs, out_specs=out_specs, check_vma=False)
```

```python
import functools
import math

import jax
import jax.numpy as jnp
import numpy as np
from jax import lax
from jax.experimental import pallas as pl
from jax.experimental.pallas import tpu as pltpu
from jax.sharding import Mesh
from jax.sharding import PartitionSpec as P

EPSILON = 1e-05
ROPE_BASE = 1000000.0
FAR = 16384.0
LANES = 128
MIB = 1024 * 1024
ALL = ("y", "x", "z", "c")
F32 = jnp.float32
BF16 = jnp.bfloat16
CORE, PLANE, FIRST_LENGTH = 0, 1, 4


def dot_nn(left, right):
    return lax.dot_general(left, right, (((1,), (0,)), ((), ())), preferred_element_type=F32)


def dot_nt(left, right):
    return lax.dot_general(left, right, (((1,), (1,)), ((), ())), preferred_element_type=F32)


def dot_tn(left, right):
    return lax.dot_general(left, right, (((0,), (0,)), ((), ())), preferred_element_type=F32)


def after(value, *needed):
    return lax.optimization_barrier((value, needed))[0]


def pick(field, index, axis=0):
    return lax.dynamic_index_in_dim(field, index, axis, keepdims=False)


def swap(field, axis_name):
    return lax.ppermute(field, axis_name, [(0, 1), (1, 0)])


def crossed(field, step, count):
    return lax.ppermute(field, "z", [(k, k ^ step) for k in range(count)])


def pair_reduce(parts, axis_name, index, *needed):
    got = after(swap(pick(parts, 1 - index), axis_name), *needed)
    return pick(parts, index) + got


def reduce_y(parts, index, *needed):
    if parts.shape[0] == 1:
        return parts[0]
    if parts.shape[0] == 2:
        return pair_reduce(parts, "y", index, *needed)
    return lax.psum_scatter(parts, "y", scatter_dimension=0, tiled=False)


class Halving:
    def __init__(self, parts, index):
        self.parts, self.index, self.step, self.count = parts, index, 1, parts.shape[0]

    def advance(self, *needed):
        far = self.parts.shape[0] // 2
        parts = self.parts.reshape(far, 2, *self.parts.shape[1:])
        bit = (self.index // self.step) % 2
        sent = pick(parts, 1 - bit, 1)
        kept = pick(parts, bit, 1)
        if needed:
            sent = after(sent, *needed)
        self.parts = kept + crossed(sent, self.step, self.count)
        self.step = self.step * 2

    def finish(self):
        while self.step < self.count:
            self.advance()
        return self.parts[0]


def in_order(index, own, other, axis):
    return jnp.concatenate(
        [jnp.where(index == 0, own, other), jnp.where(index == 0, other, own)], axis=axis)


def sum_all(vector, rows_y, rows_z):
    vector = vector + swap(vector, "c")
    vector = vector + swap(vector, "x")
    if rows_y == 2:
        vector = vector + swap(vector, "y")
    else:
        vector = lax.psum(vector, "y")
    step = 1
    while step < rows_z:
        vector = vector + crossed(vector, step, rows_z)
        step = step * 2
    return vector


def run_kernel(kernel, name, ids, operands, in_specs, out_shapes, out_specs, grid=(1,), scratch=(),
               vmem=32, micros=5, aliases=None):
    return pl.pallas_call(
        kernel,
        grid_spec=pltpu.PrefetchScalarGridSpec(
            num_scalar_prefetch=1, grid=grid, in_specs=in_specs, out_specs=out_specs,
            scratch_shapes=list(scratch)),
        out_shape=out_shapes,
        input_output_aliases=aliases or {},
        compiler_params=pltpu.CompilerParams(vmem_limit_bytes=vmem * MIB),
        cost_estimate=pl.CostEstimate(
            flops=int(micros * 1.15e9), bytes_accessed=MIB, transcendentals=0),
        name=name,
    )(ids, *operands)


def whole(shape):
    return pl.BlockSpec(tuple(shape), lambda i, ids: (0,) * len(shape))


def of_core(rows, cols):
    return pl.BlockSpec((rows, cols), lambda i, ids: (0, ids[CORE]))


def shaped(*shape, dtype=BF16):
    return jax.ShapeDtypeStruct(shape, dtype)


def lane_ids(rows):
    return lax.broadcasted_iota(jnp.int32, (rows, LANES), 1)


def half_swap(field, lanes):
    return jnp.where(
        (lanes & 63) < 32, pltpu.roll(field, LANES - 32, 1), pltpu.roll(field, 32, 1))


def half_sums(field, lanes):
    low = jnp.sum(jnp.where(lanes < 64, field, 0.0), axis=1, keepdims=True)
    high = jnp.sum(jnp.where(lanes < 64, 0.0, field), axis=1, keepdims=True)
    return jnp.where(lanes < 64, low, high)


def tables(ids, slots, first_row, rows, freq):
    token = lax.broadcasted_iota(jnp.int32, (rows, LANES), 0) + first_row
    start = jnp.zeros((rows, LANES), jnp.int32)
    edge = jnp.int32(0)
    for slot in range(slots - 1):
        edge = edge + ids[FIRST_LENGTH + slot]
        start = jnp.where(token >= edge, edge, start)
    angles = (token - start).astype(F32) * freq
    sines = jnp.sin(angles)
    return jnp.cos(angles), jnp.where((lane_ids(rows) & 63) < 32, -sines, sines)


def project_kernel(head_size, slots, ids, xo_ref, xt_ref, gain_ref, wq_ref, wk_ref, wv_ref,
                   freq_ref, qg_ref, kg_ref, ho_ref, ht_ref, *refs):
    outs, packed = refs[:-1], refs[-1]
    heads, rows, _ = packed.shape
    turn = pl.program_id(0)
    x = jnp.where(turn == 0, xo_ref[...], xt_ref[...]).astype(F32)
    scale = lax.rsqrt(jnp.mean(x * x, axis=1, keepdims=True) + EPSILON)
    h = (x * scale * gain_ref[...]).astype(BF16)

    @pl.when(turn == 0)
    def _():
        ho_ref[...] = h

    @pl.when(turn == 1)
    def _():
        ht_ref[...] = h

    lanes = lane_ids(rows)
    spot = jnp.bitwise_xor(turn, ids[CORE])
    cosine, sine = tables(ids, slots, (ids[PLANE] * 2 + spot) * rows, rows, freq_ref[...])

    def turned(raw, gain):
        unit = raw * lax.rsqrt(half_sums(raw * raw, lanes) * (1.0 / head_size) + EPSILON) * gain
        return unit * cosine + half_swap(unit, lanes) * sine

    q_raw = dot_nn(h, wq_ref[...])
    k_raw = dot_nn(h, wk_ref[...])
    v_raw = dot_nn(h, wv_ref[...])
    for head in range(heads):
        span = slice(head * LANES, (head + 1) * LANES)
        packed[head, :, 0:LANES] = turned(q_raw[:, span], qg_ref[...]).astype(BF16)
    for pair in range(heads // 2):
        span = slice(pair * LANES, (pair + 1) * LANES)
        keys = turned(k_raw[:, span], kg_ref[...])
        values = v_raw[:, span]
        even = jnp.where(lanes < 64, keys, pltpu.roll(values, 64, 1))
        odd = jnp.where(lanes < 64, pltpu.roll(keys, 64, 1), values)
        packed[2 * pair, :, LANES:] = even.astype(BF16)
        packed[2 * pair + 1, :, LANES:] = odd.astype(BF16)
    for step in range(heads):
        outs[step][...] = packed[jnp.bitwise_xor(ids[PLANE], step)]


def project(ids, x_own, x_other, gain, w_query, w_key, w_value, freq, qg, kg, head_size, slots,
            heads):
    rows, width = x_own.shape
    block = pl.BlockSpec((rows, 2 * LANES), lambda i, ids: (jnp.bitwise_xor(i, ids[CORE]), 0))
    part = whole((rows, width))
    row = whole((1, LANES))
    return run_kernel(
        functools.partial(project_kernel, head_size, slots), "project", ids,
        (x_own, x_other, gain, w_query, w_key, w_value, freq, qg, kg),
        [part, part, whole((1, width)), of_core(width, w_query.shape[1] // 2),
         of_core(width, w_key.shape[1] // 2), of_core(width, w_value.shape[1] // 2), row, row, row],
        [shaped(rows, width)] * 2 + [shaped(2 * rows, 2 * LANES)] * heads,
        [part, part] + [block] * heads,
        grid=(2,), scratch=[pltpu.VMEM((heads, rows, 2 * LANES), BF16)], vmem=32,
        micros=5)


def three_parts(value):
    high = value.astype(BF16).astype(F32)
    rest = value - high
    middle = rest.astype(BF16).astype(F32)
    return high, middle, rest - middle


def marked(lanes, first, value, otherwise):
    high, middle, low = three_parts(value)
    return jnp.where(
        lanes == first, high,
        jnp.where(lanes == first + 1, middle, jnp.where(lanes == first + 2, low, otherwise)))


def below(rows, cols):
    return lax.broadcasted_iota(jnp.int32, (rows, cols), 1) <= lax.broadcasted_iota(
        jnp.int32, (rows, cols), 0)


def attend_kernel(slots, ids, *refs):
    count = (len(refs) - 4) // 2
    arrived, sent = refs[:count], refs[count : 2 * count]
    wide_ref, qaug_ref, kaug_ref, vaug_ref = refs[2 * count :]
    block = arrived[0].shape[0]
    mark = 64 + slots
    lanes = lane_ids(block)
    plane = ids[PLANE]
    slot_lane = (lanes >= 64) & (lanes < mark)
    ones_lane = (lanes >= mark) & (lanes < mark + 3)
    for step in range(count):
        first = pl.multiple_of(jnp.bitwise_xor(plane, step) * block, block)
        span = pl.ds(first, block)
        token = lax.broadcasted_iota(jnp.int32, (block, LANES), 0) + first
        inside = lanes < 0
        edge = jnp.int32(0)
        for slot in range(slots):
            stop = edge + ids[FIRST_LENGTH + slot]
            inside = inside | ((lanes == 64 + slot) & (token >= edge) & (token < stop))
            edge = stop
        segq = jnp.where(inside, 1.0, 0.0)
        segk = jnp.where(ones_lane, 1.0, jnp.where(slot_lane & jnp.logical_not(inside), -FAR, 0.0))
        pair = arrived[step][:, 0:LANES].astype(F32)
        keyval = arrived[step][:, LANES:].astype(F32)
        qaug_ref[0, span, :] = jnp.where(lanes < 64, pair, segq).astype(BF16)
        qaug_ref[1, span, :] = jnp.where(lanes < 64, pltpu.roll(pair, 64, 1), segq).astype(BF16)
        kaug_ref[span, :] = jnp.where(lanes < 64, keyval, segk).astype(BF16)
        vaug_ref[span, :] = jnp.where(
            lanes < 64, pltpu.roll(keyval, 64, 1), jnp.where(lanes < 67, 1.0, 0.0)).astype(BF16)
    for i in range(count):
        span = slice(i * block, (i + 1) * block)
        outs = []
        for head in range(2):
            queries = qaug_ref[head, span, :]
            total = jnp.zeros((block, LANES), F32)
            for j in range(i + 1):
                other = slice(j * block, (j + 1) * block)
                weights = jnp.exp2(dot_nt(queries, kaug_ref[other, :]))
                if j == i:
                    weights = jnp.where(below(block, block), weights, 0.0)
                total = total + dot_nn(weights.astype(BF16), vaug_ref[other, :])
            row_sum = total[:, 64:65]
            outs.append(total * (1.0 / row_sum))
            qaug_ref[head, span, :] = marked(
                lanes, mark, -jnp.log2(row_sum), queries.astype(F32)).astype(BF16)
        wide_ref[span, :] = jnp.where(lanes < 64, outs[0], pltpu.roll(outs[1], 64, 1))
    for step in range(count):
        first = pl.multiple_of(jnp.bitwise_xor(plane, step) * block, block)
        sent[step][...] = wide_ref[pl.ds(first, block), :].astype(BF16)


def attend(ids, arrived, slots):
    count, block = len(arrived), arrived[0].shape[0]
    rows = count * block
    outs = [shaped(block, LANES)] * count + [
        shaped(rows, LANES, dtype=F32), shaped(2, rows, LANES), shaped(rows, LANES),
        shaped(rows, LANES)]
    return run_kernel(
        functools.partial(attend_kernel, slots), "attend", ids, arrived,
        [whole(a.shape) for a in arrived], outs, [whole(o.shape) for o in outs], vmem=40,
        micros=9)


def middle_kernel(count, ids, *refs):
    own, other = refs[:count], refs[count : 2 * count]
    xo_ref, xt_ref, w_ref, gain_ref, y_ref, ho_ref, ht_ref, o_ref = refs[2 * count :]
    turn = pl.program_id(0)
    y = jnp.where(turn == 0, xo_ref[...], xt_ref[...]).astype(F32)
    for core, blocks in ((ids[CORE], own), (1 - ids[CORE], other)):
        for step in range(count):
            head = core * count + jnp.bitwise_xor(ids[PLANE], step)
            span = pl.ds(pl.multiple_of(head * LANES, LANES), LANES)
            part = blocks[step][...]
            o_ref[:, span] = part
            y = y + dot_nn(part, w_ref[span, :])
    h = (y * lax.rsqrt(jnp.mean(y * y, axis=1, keepdims=True) + EPSILON) * gain_ref[...]).astype(
        BF16)

    @pl.when(turn == 0)
    def _():
        y_ref[...] = y
        ho_ref[...] = h

    @pl.when(turn == 1)
    def _():
        ht_ref[...] = h


def middle(ids, own, other, x_own, x_other, w_out, gain):
    rows, width = x_own.shape
    count = len(own)
    block = pl.BlockSpec((rows, LANES), lambda i, ids: (jnp.bitwise_xor(i, ids[CORE]), 0))
    part = whole((rows, width))
    return run_kernel(
        functools.partial(middle_kernel, count), "middle", ids,
        (*own, *other, x_own, x_other, w_out, gain),
        [block] * (2 * count) + [part, part, whole(w_out.shape), whole((1, width))],
        [shaped(rows, width, dtype=F32), shaped(rows, width), shaped(rows, width),
         shaped(2 * rows, width)],
        [part, part, part, pl.BlockSpec((rows, width), lambda i, ids: (i, 0))],
        grid=(2,), vmem=24, micros=4)


def feed_kernel(ids, ho_ref, ht_ref, co_ref, ct_ref, wg_ref, wu_ref, wd_ref, *refs):
    m_ref, dg_ref, du_ref, ha_ref, ca_ref, do_ref, dt_ref, yo_ref, yt_ref = refs[-9:]
    rows = ho_ref.shape[0]
    ha_ref[0:rows, :] = ho_ref[...]
    ha_ref[rows:, :] = ht_ref[...]
    ca_ref[0:rows, :] = co_ref[...]
    ca_ref[rows:, :] = ct_ref[...]
    gate = dot_nn(ha_ref[...], wg_ref[...])
    up = dot_nn(ha_ref[...], wu_ref[...])
    sig = jax.nn.sigmoid(gate)
    silu = gate * sig
    m_ref[...] = (silu * up).astype(BF16)
    dm = dot_nt(ca_ref[...], wd_ref[...])
    dg_ref[...] = (dm * up * sig * (1.0 + gate * (1.0 - sig))).astype(BF16)
    du_ref[...] = (dm * silu).astype(BF16)
    dh = dot_nt(dg_ref[...], wg_ref[...]) + dot_nt(du_ref[...], wu_ref[...])
    do_ref[...] = dh[:rows].astype(BF16)
    dt_ref[...] = dh[rows:].astype(BF16)
    y = dot_nn(m_ref[...], wd_ref[...])
    yo_ref[...] = y[:rows].astype(BF16)
    yt_ref[...] = y[rows:].astype(BF16)


def feed(ids, h_own, h_other, c_own, c_other, w_gate, w_up, w_down, earlier):
    rows, width = h_own.shape
    units = w_gate.shape[1]
    half = 1 if earlier else 0
    part = whole((rows, width))
    kept = lambda cols: pl.BlockSpec((2 * rows, cols), lambda i, ids: (half, 0))
    cols = [units] * 3 + [width] * 2
    return run_kernel(
        feed_kernel, "feed", ids, (h_own, h_other, c_own, c_other, w_gate, w_up, w_down, *earlier),
        [part] * 4 + [whole(w.shape) for w in (w_gate, w_up, w_down)]
        + [pl.BlockSpec(memory_space=pl.ANY)] * len(earlier),
        [shaped(4 * rows, n) for n in cols] + [shaped(rows, width)] * 4,
        [kept(n) for n in cols] + [part] * 4,
        vmem=44, micros=12, aliases={8 + k: k for k in range(len(earlier))})


def turn_kernel(ids, near_ref, twin_ref, far_ref, y_ref, c_ref, gain_ref, dy_ref, da_ref, sum_ref):
    y = y_ref[...]
    grad = near_ref[...].astype(F32) + twin_ref[...].astype(F32) + far_ref[...].astype(F32)
    scale = lax.rsqrt(jnp.mean(y * y, axis=1, keepdims=True) + EPSILON)
    unit = y * scale
    scaled = grad * gain_ref[...]
    inner = jnp.mean(scaled * unit, axis=1, keepdims=True)
    dy = c_ref[...].astype(F32) + scale * (scaled - unit * inner)
    dy_ref[...] = dy
    da_ref[...] = dy.astype(BF16)
    sum_ref[...] = jnp.sum(grad * unit, axis=0, keepdims=True)


def turn(ids, near, twin, far, y, c, gain):
    part, line = whole(y.shape), whole(gain.shape)
    return run_kernel(
        turn_kernel, "turn", ids, (near, twin, far, y, c, gain), [part] * 5 + [line],
        [shaped(*y.shape, dtype=F32), shaped(*y.shape), shaped(*gain.shape, dtype=F32)],
        [part, part, line], vmem=24, micros=2)


def heads_kernel(count, ids, ao_ref, at_ref, w_ref, cols_ref, *outs):
    a = jnp.where(pl.program_id(0) == 0, ao_ref[...], at_ref[...])
    half = cols_ref.shape[1]
    cols_ref[...] = jnp.where(ids[CORE] == 0, a[:, :half], a[:, half:])
    for step in range(count):
        head = ids[CORE] * count + jnp.bitwise_xor(ids[PLANE], step)
        span = pl.ds(pl.multiple_of(head * LANES, LANES), LANES)
        outs[step][...] = dot_nt(a, w_ref[span, :]).astype(BF16)


def to_heads(ids, da_own, da_other, w_out, count):
    rows, width = da_own.shape
    block = pl.BlockSpec((rows, LANES), lambda i, ids: (jnp.bitwise_xor(i, ids[CORE]), 0))
    part = whole((rows, width))
    return run_kernel(
        functools.partial(heads_kernel, count), "to_heads", ids, (da_own, da_other, w_out),
        [part, part, whole(w_out.shape)],
        [shaped(2 * rows, width // 2)] + [shaped(2 * rows, LANES)] * count,
        [pl.BlockSpec((rows, width // 2), lambda i, ids: (i, 0))] + [block] * count,
        grid=(2,), vmem=24, micros=2)


def attend_back_kernel(ids, qaug_ref, kaug_ref, vaug_ref, wide_ref, *refs):
    arrived, (dq_ref, dkv_ref, doaug, dq_sum) = refs[:-4], refs[-4:]
    count, block = len(arrived), arrived[0].shape[0]
    lanes = lane_ids(block)
    for step in range(count):
        first = pl.multiple_of(jnp.bitwise_xor(ids[PLANE], step) * block, block)
        span = pl.ds(first, block)
        do_pair = arrived[step][...].astype(F32)
        inner = do_pair * wide_ref[span, :]
        low = jnp.sum(jnp.where(lanes < 64, inner, 0.0), axis=1, keepdims=True)
        high = jnp.sum(jnp.where(lanes < 64, 0.0, inner), axis=1, keepdims=True)
        doaug[0, span, :] = jnp.where(
            lanes < 64, do_pair, marked(lanes, 64, -low, 0.0)).astype(BF16)
        doaug[1, span, :] = jnp.where(
            lanes < 64, pltpu.roll(do_pair, 64, 1), marked(lanes, 64, -high, 0.0)).astype(BF16)
    dq_sum[...] = jnp.zeros(dq_sum.shape, F32)
    for j in range(count):
        here = slice(j * block, (j + 1) * block)
        keys = kaug_ref[here, :]
        values = vaug_ref[here, :]
        dk = jnp.zeros((LANES, block), F32)
        dv = jnp.zeros((LANES, block), F32)
        for i in range(j, count):
            span = slice(i * block, (i + 1) * block)
            for head in range(2):
                queries = qaug_ref[head, span, :]
                grads = doaug[head, span, :]
                weights = jnp.exp2(dot_nt(queries, keys))
                if j == i:
                    weights = jnp.where(below(block, block), weights, 0.0)
                slopes = (weights * dot_nt(grads, values)).astype(BF16)
                dv = dv + dot_tn(grads, weights.astype(BF16))
                dk = dk + dot_tn(queries, slopes)
                dq_sum[head, span, :] = dq_sum[head, span, :] + dot_nn(slopes, keys)
        dk_rows = jnp.transpose(dk) * math.log(2.0)
        dv_rows = jnp.transpose(dv)
        dkv_ref[here, :] = jnp.where(lanes < 64, dk_rows, pltpu.roll(dv_rows, 64, 1))
    for i in range(count):
        span = slice(i * block, (i + 1) * block)
        dq_ref[span, :] = jnp.where(
            lanes < 64, dq_sum[0, span, :], pltpu.roll(dq_sum[1, span, :], 64, 1)) * 0.125


def attend_back(ids, qaug, kaug, vaug, wide, arrived):
    rows = kaug.shape[0]
    operands = (qaug, kaug, vaug, wide, *arrived)
    outs = [shaped(rows, LANES, dtype=F32)] * 2
    return run_kernel(
        attend_back_kernel, "attend_back", ids, operands, [whole(a.shape) for a in operands], outs,
        [whole(o.shape) for o in outs],
        scratch=[pltpu.VMEM((2, rows, LANES), BF16), pltpu.VMEM((2, rows, LANES), F32)], vmem=44,
        micros=13)


def pair_of(wk, wv, odd, lanes):
    keys = jnp.where(odd, pltpu.roll(wk, 64, 1), wk)
    values = jnp.where(odd, wv, pltpu.roll(wv, 64, 1))
    return jnp.where(lanes < 64, keys, values)


def unturn_kernel(head_size, ids, *refs):
    count = (len(refs) - 13) // 3
    blocks = refs[: 2 * count]
    wq_ref, wk_ref, wv_ref, cos_ref, sin_ref, qg_ref, kg_ref, dq_ref, dkv_ref = refs[
        2 * count : 2 * count + 9]
    backs = refs[2 * count + 9 : 3 * count + 9]
    grad_ref, row_ref, gains_ref, total = refs[3 * count + 9 :]
    rows = blocks[0].shape[0]
    width = wq_ref.shape[0]
    lanes = lane_ids(rows)
    odd = (ids[PLANE] & 1) == 1
    wkv = pair_of(
        wk_ref[...].astype(F32), wv_ref[...].astype(F32), odd, lane_ids(width)).astype(BF16)
    wq = wq_ref[...]

    def undo(raw, grad, gain, cosine, sine):
        scale = lax.rsqrt(half_sums(raw * raw, lanes) * (1.0 / head_size) + EPSILON)
        unit = raw * scale
        back = grad * cosine - half_swap(grad, lanes) * sine
        scaled = back * gain
        mean = half_sums(scaled * unit, lanes) * (1.0 / head_size)
        return scale * (scaled - unit * mean), jnp.sum(back * unit, axis=0, keepdims=True)

    q_gain = jnp.zeros((1, LANES), F32)
    k_gain = jnp.zeros((1, LANES), F32)
    for step in range(count):
        for twin in range(2):
            h = blocks[2 * step + twin][...]
            spot = jnp.bitwise_xor(ids[CORE], twin)
            first = pl.multiple_of(
                (jnp.bitwise_xor(ids[PLANE], step) * 2 + spot) * rows, rows)
            span = pl.ds(first, rows)
            cosine, sine = cos_ref[span, :], sin_ref[span, :]
            dkv = dkv_ref[span, :]
            dqr, add_q = undo(dot_nn(h, wq), dq_ref[span, :], qg_ref[...], cosine, sine)
            dkr, add_k = undo(
                dot_nn(h, wkv), jnp.where(lanes < 64, dkv, 0.0), kg_ref[...], cosine, sine)
            q_gain = q_gain + add_q
            k_gain = k_gain + add_k
            dqr = dqr.astype(BF16)
            dkr = jnp.where(lanes < 64, dkr, dkv).astype(BF16)
            place = pl.ds(pl.multiple_of(spot * rows, rows), rows)
            backs[step][place, 0:LANES] = dqr
            backs[step][place, LANES:] = dkr
            for at, grad in ((slice(0, LANES), dqr), (slice(LANES, 2 * LANES), dkr)):
                term = dot_tn(grad, h)
                total[at, :] = term if step + twin == 0 else total[at, :] + term
    gains_ref[...] = jnp.concatenate([q_gain, k_gain, jnp.zeros((6, LANES), F32)], axis=0)
    for at, weight in ((slice(0, LANES), wq), (slice(LANES, 2 * LANES), wkv)):
        grad_ref[:, at] = jnp.transpose(total[at, :]).astype(BF16)
    row_ref[...] = jnp.sum(
        jnp.transpose(wq.astype(F32)) * total[0:LANES, :]
        + jnp.transpose(wkv.astype(F32)) * total[LANES:, :], axis=0, keepdims=True)


def unturn(ids, blocks, w_query, w_key, w_value, cosine, sine, qg, kg, dq, dkv, head_size, heads):
    rows, width = blocks[0].shape
    count = len(blocks) // 2
    head = lambda ids: ids[CORE] * heads + ids[PLANE]
    pair = pl.BlockSpec((width, LANES), lambda i, ids: (0, head(ids) // 2))
    row = whole((1, LANES))
    outs = [shaped(2 * rows, 2 * LANES)] * count + [
        shaped(width, 2 * LANES), shaped(1, width, dtype=F32), shaped(8, LANES, dtype=F32)]
    return run_kernel(
        functools.partial(unturn_kernel, head_size), "unturn", ids,
        (*blocks, w_query, w_key, w_value, cosine, sine, qg, kg, dq, dkv),
        [whole((rows, width))] * (2 * count)
        + [pl.BlockSpec((width, LANES), lambda i, ids: (0, head(ids))), pair, pair,
           whole(cosine.shape), whole(sine.shape), row, row, whole(dq.shape), whole(dkv.shape)],
        outs, [whole(o.shape) for o in outs],
        scratch=[pltpu.VMEM((2 * LANES, width), F32)], vmem=44, micros=7)


def back_kernel(ids, *refs):
    arrived, (wq_ref, wk_ref, wv_ref, own_ref, other_ref) = refs[:-5], refs[-5:]
    rows, width = own_ref.shape
    total = [jnp.zeros((rows, width), F32)] * 2
    for step in range(len(arrived)):
        head = jnp.bitwise_xor(ids[PLANE], step)
        span = pl.ds(pl.multiple_of(head * LANES, LANES), LANES)
        both = pl.ds(pl.multiple_of(head // 2 * LANES, LANES), LANES)
        wkv = pair_of(wk_ref[:, both].astype(F32), wv_ref[:, both].astype(F32), (head & 1) == 1,
                      lane_ids(width)).astype(BF16)
        wq = wq_ref[:, span]
        for twin in range(2):
            spot = jnp.bitwise_xor(ids[CORE], twin)
            grads = arrived[step][pl.ds(pl.multiple_of(spot * rows, rows), rows), :]
            total[twin] = total[twin] + dot_nt(grads[:, :LANES], wq) + dot_nt(grads[:, LANES:], wkv)
    own_ref[...] = total[0].astype(BF16)
    other_ref[...] = total[1].astype(BF16)


def to_tokens(ids, arrived, w_query, w_key, w_value):
    width = w_query.shape[0]
    rows = arrived[0].shape[0] // 2
    return run_kernel(
        back_kernel, "to_tokens", ids, (*arrived, w_query, w_key, w_value),
        [whole(a.shape) for a in arrived]
        + [of_core(width, w.shape[1] // 2) for w in (w_query, w_key, w_value)],
        [shaped(rows, width)] * 2, [whole((rows, width))] * 2, vmem=24, micros=4)


def last_kernel(ids, mine_ref, twin_ref, x_ref, dy_ref, gain_ref, out_ref):
    x = x_ref[...].astype(F32)
    scaled = (mine_ref[...].astype(F32) + twin_ref[...].astype(F32)) * gain_ref[...]
    scale = lax.rsqrt(jnp.mean(x * x, axis=1, keepdims=True) + EPSILON)
    unit = x * scale
    inner = jnp.mean(scaled * unit, axis=1, keepdims=True)
    out_ref[...] = dy_ref[...] + scale * (scaled - unit * inner)


def last(ids, mine, twin, x, dy, gain):
    part = whole(x.shape)
    return run_kernel(
        last_kernel, "last", ids, (mine, twin, x, dy, gain), [part] * 4 + [whole(gain.shape)],
        shaped(*x.shape, dtype=F32), part, vmem=24, micros=2)


def body(tokens, lengths, attn_gain, w_query, w_key, w_value, query_gain, key_gain, w_out,
         ffn_gain, w_gate, w_up, w_down, cotangent):
    rows, width = tokens.shape
    head_size = query_gain.shape[0]
    n_y, n_z = lax.axis_size("y"), lax.axis_size("z")
    i_y, i_x, i_z, i_c = (lax.axis_index(name) for name in ALL)
    heads = w_key.shape[1] // head_size // 2
    slots = lengths.shape[1]
    ids = jnp.concatenate(
        [jnp.stack([i_c, i_z, i_x, i_y]).astype(jnp.int32), lengths[0].astype(jnp.int32)])
    lane = np.arange(LANES)
    freq = jnp.asarray(
        (ROPE_BASE ** (-2.0 * (lane % (head_size // 2)) / head_size)).astype(np.float32))[None, :]
    to_exp2 = math.log2(math.e) / math.sqrt(head_size)
    qg = jnp.tile(query_gain, 2)[None, :]
    kg = jnp.tile(key_gain, 2)[None, :]
    a_gain, f_gain = attn_gain[None, :], ffn_gain[None, :]
    steps = range(1, n_z)

    x_other = swap(tokens, "c")
    h_own, h_other, *packed = project(
        ids, tokens, x_other, a_gain, w_query, w_key, w_value, freq, qg * to_exp2, kg, head_size,
        slots, heads)
    arrived = [packed[0]] + [crossed(packed[s], s, n_z) for s in steps]

    cot, lengths_late, *w_late = after(
        (cotangent, lengths, w_gate, w_up, w_down), packed[0])
    cot_other = swap(cot, "c")
    cot_far = swap(cot, "x")
    cot_far_other = swap(cot_far, "c")
    units = w_gate.shape[1] // 4
    place = (2 * i_x + i_c) * units
    wg, wu = (lax.dynamic_slice_in_dim(w, place, units, 1) for w in w_late[:2])
    wd = lax.dynamic_slice_in_dim(w_late[2], place, units, 0)
    token = jnp.arange(2 * rows * n_z, dtype=jnp.int32)
    start, edge = jnp.zeros_like(token), jnp.zeros((), jnp.int32)
    for slot in range(slots - 1):
        edge = edge + lengths_late[0, slot]
        start = jnp.where(token >= edge, edge, start)
    angles = (token - start).astype(F32)[:, None] * freq
    sign = jnp.asarray(np.where(lane % head_size < head_size // 2, -1.0, 1.0).astype(np.float32))
    cosine, sine = jnp.cos(angles), jnp.sin(angles) * sign[None, :]

    *o_sent, wide, qaug, kaug, vaug = attend(ids, arrived, slots)
    o_own = [o_sent[0]] + [crossed(o_sent[s], s, n_z) for s in steps]
    o_other = [swap(o, "c") for o in o_own]
    y_mine, h2_own, h2_other, o_rows = middle(
        ids, o_own, o_other, tokens, x_other, w_out, f_gain)

    h_line = after(h_own, o_own[-1])
    blocks = [h_own, h_other]
    for s in steps:
        one = crossed(h_line, s, n_z)
        blocks += [one, swap(one, "c")]

    h2_far = swap(h2_own, "x")
    *kept, d_own, d_other, y_own, y_other = feed(
        ids, h2_own, h2_other, cot, cot_other, wg, wu, wd, ())
    h2_far_other = swap(after(h2_far, d_own), "c")
    d_twin = swap(d_other, "c")
    *kept, d_far, d_far_other, y_far, y_far_other = feed(
        ids, h2_far, h2_far_other, cot_far, cot_far_other, wg, wu, wd, tuple(kept))
    d_home = swap(d_far + swap(d_far_other, "c"), "x")

    m, dg, du, h2_all, cot_all = kept
    piece = units // (n_y * n_z)
    row_block = width // (n_y * 2 * n_z * 2)
    m, dg, du = after((m, dg, du), d_far_other, *blocks[2:])

    dy, da, gain_ffn = turn(ids, d_own, d_twin, d_home, y_mine, cotangent, f_gain)
    da_other = swap(da, "c")
    da_cols, *do_sent = to_heads(ids, da, da_other, w_out, heads)
    do_arrived = [do_sent[0]] + [crossed(do_sent[s], s, n_z) for s in steps]
    dq, dkv = attend_back(ids, qaug, kaug, vaug, wide, do_arrived)

    down = dot_tn(m, cot_all).astype(BF16).reshape(n_z, n_y, piece, width)
    down = Halving(reduce_y(jnp.moveaxis(down, 1, 0), i_y, do_sent[0]), i_z)

    def over_y(grad, *needed):
        grad = grad.astype(BF16).reshape(n_y, 2, n_z, 2, row_block, -1)
        return Halving(jnp.moveaxis(reduce_y(grad, i_y, *needed), 1, 0), i_z)

    down.advance(do_arrived[-1])
    out_parts = dot_tn(o_rows, after(da_cols, do_sent[0])).astype(BF16).reshape(
        n_y, 2, n_z, 2, row_block, width // 2)
    out_parts = pair_reduce(jnp.moveaxis(out_parts, 1, 0), "x", i_x, dq)

    *back, grad_head, gain_attn, gains = unturn(
        ids, blocks, w_query, w_key, w_value, cosine, sine, qg, kg, dq, dkv, head_size, heads)
    back_arrived = [back[0]] + [crossed(back[s], s, n_z) for s in steps]
    late = back_arrived[-1]
    gate = over_y(dot_tn(h2_all, dg), back[0])
    up = over_y(dot_tn(h2_all, du), late)
    down.advance(dq)
    gate.advance()
    dh_own, dh_other = to_tokens(ids, back_arrived, w_query, w_key, w_value)
    grad_tokens = last(ids, dh_own, swap(dh_other, "c"), tokens, dy, a_gain)

    gate.advance(late)
    up.advance()
    owners = []
    for y in range(n_y):
        for x in range(2):
            for z in range(n_z):
                for c in range(2):
                    source = ((y * 2 + x) * n_z + z) * 2 + c
                    owners.append((source, n_y * n_z * (2 * x + c) + z * n_y + y))
    share_down = lax.ppermute(after(down.finish(), late), ALL, owners).astype(F32)

    def spread(parts):
        got = swap(pick(parts, 1 - i_c, 1), "c")
        cols = in_order(i_c, pick(parts, i_c, 1), got, 2)
        got = swap(pick(cols, 1 - i_x), "x")
        return in_order(i_x, pick(cols, i_x), got, 1).astype(F32)

    share_gate = spread(gate.finish())
    share_up = spread(up.finish())

    parts = after(grad_head, back[0]).reshape(n_y, 2, n_z, 2, row_block, 2 * LANES)
    parts = pair_reduce(jnp.moveaxis(parts, 1, 0), "x", i_x, late)
    half = width // 2
    parts = reduce_y(jnp.concatenate([out_parts, parts], axis=-1), i_y)
    got = [pick(parts, i_z)] + [crossed(pick(parts, i_z ^ s), s, n_z) for s in steps]
    out_sum = got[0][..., :half].astype(F32)
    for one in got[1:]:
        out_sum = out_sum + one[..., :half].astype(F32)
    by_step = jnp.stack(got)[..., half:]
    merged = jnp.concatenate(
        [out_sum.astype(BF16)] + [pick(by_step, i_z ^ z) for z in range(n_z)], axis=-1)
    kept_c, got = pick(merged, i_c), swap(pick(merged, 1 - i_c), "c")
    share_out = in_order(i_c, kept_c[:, :half], got[:, :half], 1).astype(F32)
    by_head = in_order(i_c, kept_c[:, half:], got[:, half:], 1).astype(F32)
    by_head = by_head.reshape(row_block, 2 * heads, 2 * LANES)
    share_query = by_head[:, :, :LANES].reshape(row_block, -1)
    share_key = by_head[:, :, LANES : LANES + head_size].reshape(row_block, -1)
    share_value = by_head[:, :, LANES + head_size :].reshape(row_block, -1)

    y_own, y_other, y_far, y_far_other = after((y_own, y_other, y_far, y_far_other), do_sent[0])
    y_home = swap(y_far + swap(y_far_other, "c"), "x")
    y_sum = y_own.astype(F32) + swap(y_other, "c").astype(F32) + y_home.astype(F32)
    mixed = (y_mine + y_sum).astype(BF16)

    sums = sum_all(
        after(jnp.concatenate(
            [gain_attn / a_gain, gain_ffn, gains[0:1, :head_size] + gains[0:1, head_size:],
             gains[1:2, :head_size]], axis=1), late), n_y, n_z)[0]
    return (
        mixed,
        grad_tokens,
        sums[:width],
        share_query,
        share_key,
        share_value,
        sums[2 * width : 2 * width + head_size],
        sums[2 * width + head_size :],
        share_out,
        sums[width : 2 * width],
        share_gate,
        share_up,
        share_down,
    )


def solution(mesh):
    n_dp, n_seq = mesh.shape["dp"], mesh.shape["seq"]
    fine = Mesh(mesh.devices.reshape(n_dp // 2, 2, n_seq // 2, 2), ALL)
    split = P(ALL, None)
    in_specs = (split, P(("y", "x"), None)) + (P(),) * 11 + (split,)
    out_specs = (split, split, P(), split, split, split, P(), P(), split, P(), split, split, split)
    return jax.shard_map(body, mesh=fine, in_specs=in_specs, out_specs=out_specs, check_vma=False)
```

```python
import functools
import math

import jax
import jax.numpy as jnp
import numpy as np
from jax import lax
from jax.experimental import pallas as pl
from jax.experimental.pallas import tpu as pltpu
from jax.sharding import Mesh
from jax.sharding import PartitionSpec as P

EPSILON = 1e-05
ROPE_BASE = 1000000.0
FAR = 16384.0
LANES = 128
MIB = 1024 * 1024
ALL = ("y", "x", "z", "c")
F32 = jnp.float32
BF16 = jnp.bfloat16
CORE, PLANE, FIRST_LENGTH = 0, 1, 4


def dot_nn(left, right):
    return lax.dot_general(left, right, (((1,), (0,)), ((), ())), preferred_element_type=F32)


def dot_nt(left, right):
    return lax.dot_general(left, right, (((1,), (1,)), ((), ())), preferred_element_type=F32)


def dot_tn(left, right):
    return lax.dot_general(left, right, (((0,), (0,)), ((), ())), preferred_element_type=F32)


def after(value, *needed):
    return lax.optimization_barrier((value, needed))[0]


def pick(field, index, axis=0):
    return lax.dynamic_index_in_dim(field, index, axis, keepdims=False)


def swap(field, axis_name):
    return lax.ppermute(field, axis_name, [(0, 1), (1, 0)])


def crossed(field, step, count):
    return lax.ppermute(field, "z", [(k, k ^ step) for k in range(count)])


def along(to_right, to_left, count):
    pairs = range(count - 1)
    return (lax.ppermute(to_right, "z", [(k, k + 1) for k in pairs]),
            lax.ppermute(to_left, "z", [(k + 1, k) for k in pairs]))


class Pair:
    def __init__(self, parts, index, *needed, axis_name="y"):
        self.parts, self.index, self.sent, self.got = parts, index, parts, None
        if parts.shape[0] == 2:
            self.sent = after(pick(parts, 1 - index), *needed)
            self.got = swap(self.sent, axis_name)

    def finish(self, *needed):
        if self.parts.shape[0] == 1:
            return self.parts[0]
        if self.got is None:
            return lax.psum_scatter(self.parts, "y", scatter_dimension=0, tiled=False)
        return pick(self.parts, self.index) + after(self.got, *needed)


class Halving:
    def __init__(self, parts, index):
        self.parts, self.index, self.step, self.count = parts, index, 1, parts.shape[0]

    def advance(self, *needed):
        far = self.parts.shape[0] // 2
        parts = self.parts.reshape(far, 2, *self.parts.shape[1:])
        bit = (self.index // self.step) % 2
        sent = pick(parts, 1 - bit, 1)
        kept = pick(parts, bit, 1)
        if needed:
            sent = after(sent, *needed)
        self.sent = sent
        self.parts = kept + crossed(sent, self.step, self.count)
        self.step = self.step * 2

    def finish(self):
        while self.step < self.count:
            self.advance()
        return self.parts[0]


def in_order(index, own, other, axis):
    return jnp.concatenate(
        [jnp.where(index == 0, own, other), jnp.where(index == 0, other, own)], axis=axis)


def split_up(field):
    high = field.astype(BF16)
    rest = field - high.astype(F32)
    middle = rest.astype(BF16)
    return [high, middle, (rest - middle.astype(F32)).astype(BF16)]


def run_kernel(kernel, name, ids, operands, in_specs, out_shapes, out_specs, grid=(1,), scratch=(),
               vmem=32, micros=5, aliases=None):
    return pl.pallas_call(
        kernel,
        grid_spec=pltpu.PrefetchScalarGridSpec(
            num_scalar_prefetch=1, grid=grid, in_specs=in_specs, out_specs=out_specs,
            scratch_shapes=list(scratch)),
        out_shape=out_shapes,
        input_output_aliases=aliases or {},
        compiler_params=pltpu.CompilerParams(vmem_limit_bytes=vmem * MIB),
        cost_estimate=pl.CostEstimate(
            flops=int(micros * 1e5), bytes_accessed=1024, transcendentals=0),
        name=name,
    )(ids, *operands)


def whole(shape):
    return pl.BlockSpec(tuple(shape), lambda i, ids: (0,) * len(shape))


def of_core(rows, cols):
    return pl.BlockSpec((rows, cols), lambda i, ids: (0, ids[CORE]))


def shaped(*shape, dtype=BF16):
    return jax.ShapeDtypeStruct(shape, dtype)


def lane_ids(rows):
    return lax.broadcasted_iota(jnp.int32, (rows, LANES), 1)


def half_swap(field, lanes):
    return jnp.where(
        (lanes & 63) < 32, pltpu.roll(field, LANES - 32, 1), pltpu.roll(field, 32, 1))


def half_sums(field, lanes):
    low = jnp.sum(jnp.where(lanes < 64, field, 0.0), axis=1, keepdims=True)
    high = jnp.sum(jnp.where(lanes < 64, 0.0, field), axis=1, keepdims=True)
    return jnp.where(lanes < 64, low, high)


def tables(ids, slots, first_row, rows, freq):
    token = lax.broadcasted_iota(jnp.int32, (rows, LANES), 0) + first_row
    start = jnp.zeros((rows, LANES), jnp.int32)
    edge = jnp.int32(0)
    for slot in range(slots - 1):
        edge = edge + ids[FIRST_LENGTH + slot]
        start = jnp.where(token >= edge, edge, start)
    angles = (token - start).astype(F32) * freq
    sines = jnp.sin(angles)
    return jnp.cos(angles), jnp.where((lane_ids(rows) & 63) < 32, -sines, sines)


def project_kernel(head_size, slots, ids, xo_ref, xt_ref, gain_ref, wq_ref, wk_ref, wv_ref,
                   freq_ref, qg_ref, kg_ref, ho_ref, ht_ref, *refs):
    outs, packed = refs[:-1], refs[-1]
    heads, rows, _ = packed.shape
    turn = pl.program_id(0)
    x = jnp.where(turn == 0, xo_ref[...], xt_ref[...]).astype(F32)
    scale = lax.rsqrt(jnp.mean(x * x, axis=1, keepdims=True) + EPSILON)
    h = (x * scale * gain_ref[...]).astype(BF16)

    @pl.when(turn == 0)
    def _():
        ho_ref[...] = h

    @pl.when(turn == 1)
    def _():
        ht_ref[...] = h

    lanes = lane_ids(rows)
    spot = jnp.bitwise_xor(turn, ids[CORE])
    cosine, sine = tables(ids, slots, (ids[PLANE] * 2 + spot) * rows, rows, freq_ref[...])

    def turned(raw, gain):
        unit = raw * lax.rsqrt(half_sums(raw * raw, lanes) * (1.0 / head_size) + EPSILON) * gain
        return unit * cosine + half_swap(unit, lanes) * sine

    q_raw = dot_nn(h, wq_ref[...])
    k_raw = dot_nn(h, wk_ref[...])
    v_raw = dot_nn(h, wv_ref[...])
    for head in range(heads):
        span = slice(head * LANES, (head + 1) * LANES)
        packed[head, :, 0:LANES] = turned(q_raw[:, span], qg_ref[...]).astype(BF16)
    for pair in range(heads // 2):
        span = slice(pair * LANES, (pair + 1) * LANES)
        keys = turned(k_raw[:, span], kg_ref[...])
        values = v_raw[:, span]
        even = jnp.where(lanes < 64, keys, pltpu.roll(values, 64, 1))
        odd = jnp.where(lanes < 64, pltpu.roll(keys, 64, 1), values)
        packed[2 * pair, :, LANES:] = even.astype(BF16)
        packed[2 * pair + 1, :, LANES:] = odd.astype(BF16)
    for step in range(heads):
        outs[step][...] = packed[jnp.bitwise_xor(ids[PLANE], step)]


def project(ids, x_own, x_other, gain, w_query, w_key, w_value, freq, qg, kg, head_size, slots,
            heads):
    rows, width = x_own.shape
    block = pl.BlockSpec((rows, 2 * LANES), lambda i, ids: (jnp.bitwise_xor(i, ids[CORE]), 0))
    part = whole((rows, width))
    row = whole((1, LANES))
    return run_kernel(
        functools.partial(project_kernel, head_size, slots), "project", ids,
        (x_own, x_other, gain, w_query, w_key, w_value, freq, qg, kg),
        [part, part, whole((1, width)), of_core(width, w_query.shape[1] // 2),
         of_core(width, w_key.shape[1] // 2), of_core(width, w_value.shape[1] // 2), row, row, row],
        [shaped(rows, width)] * 2 + [shaped(2 * rows, 2 * LANES)] * heads,
        [part, part] + [block] * heads,
        grid=(2,), scratch=[pltpu.VMEM((heads, rows, 2 * LANES), BF16)], vmem=58,
        micros=5)


def three_parts(value):
    high = value.astype(BF16).astype(F32)
    rest = value - high
    middle = rest.astype(BF16).astype(F32)
    return high, middle, rest - middle


def marked(lanes, first, value, otherwise):
    high, middle, low = three_parts(value)
    return jnp.where(
        lanes == first, high,
        jnp.where(lanes == first + 1, middle, jnp.where(lanes == first + 2, low, otherwise)))


def below(rows, cols):
    return lax.broadcasted_iota(jnp.int32, (rows, cols), 1) <= lax.broadcasted_iota(
        jnp.int32, (rows, cols), 0)


def attend_kernel(slots, ids, *refs):
    count = (len(refs) - 4) // 2
    arrived, sent = refs[:count], refs[count : 2 * count]
    wide_ref, qaug_ref, kaug_ref, vaug_ref = refs[2 * count :]
    block = arrived[0].shape[0]
    mark = 64 + slots
    lanes = lane_ids(block)
    plane = ids[PLANE]
    slot_lane = (lanes >= 64) & (lanes < mark)
    ones_lane = (lanes >= mark) & (lanes < mark + 3)
    for step in range(count):
        first = pl.multiple_of(jnp.bitwise_xor(plane, step) * block, block)
        span = pl.ds(first, block)
        token = lax.broadcasted_iota(jnp.int32, (block, LANES), 0) + first
        inside = lanes < 0
        edge = jnp.int32(0)
        for slot in range(slots):
            stop = edge + ids[FIRST_LENGTH + slot]
            inside = inside | ((lanes == 64 + slot) & (token >= edge) & (token < stop))
            edge = stop
        segq = jnp.where(inside, 1.0, 0.0)
        segk = jnp.where(ones_lane, 1.0, jnp.where(slot_lane & jnp.logical_not(inside), -FAR, 0.0))
        pair = arrived[step][:, 0:LANES].astype(F32)
        keyval = arrived[step][:, LANES:].astype(F32)
        qaug_ref[0, span, :] = jnp.where(lanes < 64, pair, segq).astype(BF16)
        qaug_ref[1, span, :] = jnp.where(lanes < 64, pltpu.roll(pair, 64, 1), segq).astype(BF16)
        kaug_ref[span, :] = jnp.where(lanes < 64, keyval, segk).astype(BF16)
        vaug_ref[span, :] = jnp.where(
            lanes < 64, pltpu.roll(keyval, 64, 1), jnp.where(lanes < 67, 1.0, 0.0)).astype(BF16)
    for i in range(count):
        span = slice(i * block, (i + 1) * block)
        outs = []
        for head in range(2):
            queries = qaug_ref[head, span, :]
            total = jnp.zeros((block, LANES), F32)
            for j in range(i + 1):
                other = slice(j * block, (j + 1) * block)
                weights = jnp.exp2(dot_nt(queries, kaug_ref[other, :]))
                if j == i:
                    weights = jnp.where(below(block, block), weights, 0.0)
                total = total + dot_nn(weights.astype(BF16), vaug_ref[other, :])
            row_sum = total[:, 64:65]
            outs.append(total * (1.0 / row_sum))
            qaug_ref[head, span, :] = marked(
                lanes, mark, -jnp.log2(row_sum), queries.astype(F32)).astype(BF16)
        wide_ref[span, :] = jnp.where(lanes < 64, outs[0], pltpu.roll(outs[1], 64, 1))
    for step in range(count):
        first = pl.multiple_of(jnp.bitwise_xor(plane, step) * block, block)
        sent[step][...] = wide_ref[pl.ds(first, block), :].astype(BF16)


def attend(ids, arrived, slots):
    count, block = len(arrived), arrived[0].shape[0]
    rows = count * block
    outs = [shaped(block, LANES)] * count + [
        shaped(rows, LANES, dtype=F32), shaped(2, rows, LANES), shaped(rows, LANES),
        shaped(rows, LANES)]
    return run_kernel(
        functools.partial(attend_kernel, slots), "attend", ids, arrived,
        [whole(a.shape) for a in arrived], outs, [whole(o.shape) for o in outs], vmem=40,
        micros=9)


def middle_kernel(count, ids, *refs):
    own, other = refs[:count], refs[count : 2 * count]
    xo_ref, xt_ref, w_ref, gain_ref, y_ref, ho_ref, ht_ref, o_ref = refs[2 * count :]
    turn = pl.program_id(0)
    for core, blocks in ((ids[CORE], own), (1 - ids[CORE], other)):
        for step in range(count):
            head = core * count + jnp.bitwise_xor(ids[PLANE], step)
            o_ref[:, pl.ds(pl.multiple_of(head * LANES, LANES), LANES)] = blocks[step][...]
    y = jnp.where(turn == 0, xo_ref[...], xt_ref[...]).astype(F32)
    y = y + dot_nn(o_ref[...], w_ref[...])
    h = (y * lax.rsqrt(jnp.mean(y * y, axis=1, keepdims=True) + EPSILON) * gain_ref[...]).astype(
        BF16)

    @pl.when(turn == 0)
    def _():
        y_ref[...] = y
        ho_ref[...] = h

    @pl.when(turn == 1)
    def _():
        ht_ref[...] = h


def middle(ids, own, other, x_own, x_other, w_out, gain):
    rows, width = x_own.shape
    count = len(own)
    block = pl.BlockSpec((rows, LANES), lambda i, ids: (jnp.bitwise_xor(i, ids[CORE]), 0))
    part = whole((rows, width))
    return run_kernel(
        functools.partial(middle_kernel, count), "middle", ids,
        (*own, *other, x_own, x_other, w_out, gain),
        [block] * (2 * count) + [part, part, whole(w_out.shape), whole((1, width))],
        [shaped(rows, width, dtype=F32), shaped(rows, width), shaped(rows, width),
         shaped(2 * rows, width)],
        [part, part, part, pl.BlockSpec((rows, width), lambda i, ids: (i, 0))],
        grid=(2,), vmem=58, micros=4)


def feed_kernel(ids, ho_ref, ht_ref, co_ref, ct_ref, wg_all, wu_all, wd_all, *refs):
    m_ref, dg_ref, du_ref, ha_ref, ca_ref, do_ref, dt_ref, yo_ref, yt_ref = refs[-13:-4]
    wg_ref, wu_ref, wd_ref, arrivals = refs[-4:]
    rows = ho_ref.shape[0]
    units = wg_ref.shape[1]
    mine = pl.ds(pl.multiple_of((2 * ids[2] + ids[CORE]) * units, LANES), units)
    gates = pltpu.make_async_copy(wg_all.at[:, mine], wg_ref, arrivals.at[0])
    ups = pltpu.make_async_copy(wu_all.at[:, mine], wu_ref, arrivals.at[1])
    downs = pltpu.make_async_copy(wd_all.at[mine, :], wd_ref, arrivals.at[2])
    gates.start()
    ups.start()
    downs.start()
    ha_ref[0:rows, :] = ho_ref[...]
    ha_ref[rows:, :] = ht_ref[...]
    ca_ref[0:rows, :] = co_ref[...]
    ca_ref[rows:, :] = ct_ref[...]
    gates.wait()
    gate = dot_nn(ha_ref[...], wg_ref[...])
    ups.wait()
    up = dot_nn(ha_ref[...], wu_ref[...])
    downs.wait()
    sig = jax.nn.sigmoid(gate)
    silu = gate * sig
    m_ref[...] = (silu * up).astype(BF16)
    dm = dot_nt(ca_ref[...], wd_ref[...])
    dg_ref[...] = (dm * up * sig * (1.0 + gate * (1.0 - sig))).astype(BF16)
    du_ref[...] = (dm * silu).astype(BF16)
    dh = dot_nt(dg_ref[...], wg_ref[...]) + dot_nt(du_ref[...], wu_ref[...])
    do_ref[...] = dh[:rows].astype(BF16)
    dt_ref[...] = dh[rows:].astype(BF16)
    y = dot_nn(m_ref[...], wd_ref[...])
    yo_ref[...] = y[:rows].astype(BF16)
    yt_ref[...] = y[rows:].astype(BF16)


def feed(ids, h_own, h_other, c_own, c_other, w_gate, w_up, w_down, earlier, units):
    rows, width = h_own.shape
    half = 1 if earlier else 0
    part = whole((rows, width))
    anywhere = pl.BlockSpec(memory_space=pl.ANY)
    kept = lambda cols: pl.BlockSpec((2 * rows, cols), lambda i, ids: (half, 0))
    cols = [units] * 3 + [width] * 2
    return run_kernel(
        feed_kernel, "feed", ids, (h_own, h_other, c_own, c_other, w_gate, w_up, w_down, *earlier),
        [part] * 4 + [anywhere] * (3 + len(earlier)),
        [shaped(4 * rows, n) for n in cols] + [shaped(rows, width)] * 4,
        [kept(n) for n in cols] + [part] * 4,
        scratch=[pltpu.VMEM((width, units), BF16)] * 2
        + [pltpu.VMEM((units, width), BF16), pltpu.SemaphoreType.DMA((3,))],
        vmem=58, micros=12, aliases={8 + k: k for k in range(len(earlier))})


def turn_kernel(ids, near_ref, twin_ref, far_ref, y_ref, c_ref, gain_ref, dy_ref, da_ref, sum_ref):
    y = y_ref[...]
    grad = near_ref[...].astype(F32) + twin_ref[...].astype(F32) + far_ref[...].astype(F32)
    scale = lax.rsqrt(jnp.mean(y * y, axis=1, keepdims=True) + EPSILON)
    unit = y * scale
    scaled = grad * gain_ref[...]
    inner = jnp.mean(scaled * unit, axis=1, keepdims=True)
    dy = c_ref[...].astype(F32) + scale * (scaled - unit * inner)
    dy_ref[...] = dy
    da_ref[...] = dy.astype(BF16)
    sum_ref[...] = jnp.sum(grad * unit, axis=0, keepdims=True)


def turn(ids, near, twin, far, y, c, gain):
    part, line = whole(y.shape), whole(gain.shape)
    return run_kernel(
        turn_kernel, "turn", ids, (near, twin, far, y, c, gain), [part] * 5 + [line],
        [shaped(*y.shape, dtype=F32), shaped(*y.shape), shaped(*gain.shape, dtype=F32)],
        [part, part, line], vmem=24, micros=2)


def heads_kernel(count, ids, ao_ref, at_ref, w_ref, cols_ref, *outs):
    a = jnp.where(pl.program_id(0) == 0, ao_ref[...], at_ref[...])
    half = cols_ref.shape[1]
    cols_ref[...] = jnp.where(ids[CORE] == 0, a[:, :half], a[:, half:])
    for step in range(count):
        head = ids[CORE] * count + jnp.bitwise_xor(ids[PLANE], step)
        span = pl.ds(pl.multiple_of(head * LANES, LANES), LANES)
        outs[step][...] = dot_nt(a, w_ref[span, :]).astype(BF16)


def to_heads(ids, da_own, da_other, w_out, count):
    rows, width = da_own.shape
    block = pl.BlockSpec((rows, LANES), lambda i, ids: (jnp.bitwise_xor(i, ids[CORE]), 0))
    part = whole((rows, width))
    return run_kernel(
        functools.partial(heads_kernel, count), "to_heads", ids, (da_own, da_other, w_out),
        [part, part, whole(w_out.shape)],
        [shaped(2 * rows, width // 2)] + [shaped(2 * rows, LANES)] * count,
        [pl.BlockSpec((rows, width // 2), lambda i, ids: (i, 0))] + [block] * count,
        grid=(2,), vmem=58, micros=2)


def attend_back_kernel(ids, qaug_ref, kaug_ref, vaug_ref, wide_ref, *refs):
    arrived, (dq_ref, dkv_ref, doaug, dq_sum) = refs[:-4], refs[-4:]
    count, block = len(arrived), arrived[0].shape[0]
    lanes = lane_ids(block)
    for step in range(count):
        first = pl.multiple_of(jnp.bitwise_xor(ids[PLANE], step) * block, block)
        span = pl.ds(first, block)
        do_pair = arrived[step][...].astype(F32)
        inner = do_pair * wide_ref[span, :]
        low = jnp.sum(jnp.where(lanes < 64, inner, 0.0), axis=1, keepdims=True)
        high = jnp.sum(jnp.where(lanes < 64, 0.0, inner), axis=1, keepdims=True)
        doaug[0, span, :] = jnp.where(
            lanes < 64, do_pair, marked(lanes, 64, -low, 0.0)).astype(BF16)
        doaug[1, span, :] = jnp.where(
            lanes < 64, pltpu.roll(do_pair, 64, 1), marked(lanes, 64, -high, 0.0)).astype(BF16)
    dq_sum[...] = jnp.zeros(dq_sum.shape, F32)
    for j in range(count):
        here = slice(j * block, (j + 1) * block)
        keys = kaug_ref[here, :]
        values = vaug_ref[here, :]
        dk = jnp.zeros((LANES, block), F32)
        dv = jnp.zeros((LANES, block), F32)
        for i in range(j, count):
            span = slice(i * block, (i + 1) * block)
            for head in range(2):
                queries = qaug_ref[head, span, :]
                grads = doaug[head, span, :]
                weights = jnp.exp2(dot_nt(queries, keys))
                if j == i:
                    weights = jnp.where(below(block, block), weights, 0.0)
                slopes = (weights * dot_nt(grads, values)).astype(BF16)
                dv = dv + dot_tn(grads, weights.astype(BF16))
                dk = dk + dot_tn(queries, slopes)
                dq_sum[head, span, :] = dq_sum[head, span, :] + dot_nn(slopes, keys)
        dk_rows = jnp.transpose(dk) * math.log(2.0)
        dv_rows = jnp.transpose(dv)
        dkv_ref[here, :] = jnp.where(lanes < 64, dk_rows, pltpu.roll(dv_rows, 64, 1))
    for i in range(count):
        span = slice(i * block, (i + 1) * block)
        dq_ref[span, :] = jnp.where(
            lanes < 64, dq_sum[0, span, :], pltpu.roll(dq_sum[1, span, :], 64, 1)) * 0.125


def attend_back(ids, qaug, kaug, vaug, wide, arrived):
    rows = kaug.shape[0]
    operands = (qaug, kaug, vaug, wide, *arrived)
    outs = [shaped(rows, LANES, dtype=F32)] * 2
    return run_kernel(
        attend_back_kernel, "attend_back", ids, operands, [whole(a.shape) for a in operands], outs,
        [whole(o.shape) for o in outs],
        scratch=[pltpu.VMEM((2, rows, LANES), BF16), pltpu.VMEM((2, rows, LANES), F32)], vmem=44,
        micros=13)


def pair_of(wk, wv, odd, lanes):
    keys = jnp.where(odd, pltpu.roll(wk, 64, 1), wk)
    values = jnp.where(odd, wv, pltpu.roll(wv, 64, 1))
    return jnp.where(lanes < 64, keys, values)


def unturn_kernel(head_size, ids, *refs):
    count = (len(refs) - 13) // 3
    blocks = refs[: 2 * count]
    wq_ref, wk_ref, wv_ref, cos_ref, sin_ref, qg_ref, kg_ref, dq_ref, dkv_ref = refs[
        2 * count : 2 * count + 9]
    backs = refs[2 * count + 9 : 3 * count + 9]
    grad_ref, row_ref, gains_ref, total = refs[3 * count + 9 :]
    rows = blocks[0].shape[0]
    width = wq_ref.shape[0]
    lanes = lane_ids(rows)
    odd = (ids[PLANE] & 1) == 1
    wkv = pair_of(
        wk_ref[...].astype(F32), wv_ref[...].astype(F32), odd, lane_ids(width)).astype(BF16)
    wq = wq_ref[...]

    def undo(raw, grad, gain, cosine, sine):
        scale = lax.rsqrt(half_sums(raw * raw, lanes) * (1.0 / head_size) + EPSILON)
        unit = raw * scale
        back = grad * cosine - half_swap(grad, lanes) * sine
        scaled = back * gain
        mean = half_sums(scaled * unit, lanes) * (1.0 / head_size)
        return scale * (scaled - unit * mean), jnp.sum(back * unit, axis=0, keepdims=True)

    q_gain = jnp.zeros((1, LANES), F32)
    k_gain = jnp.zeros((1, LANES), F32)
    for step in range(count):
        for twin in range(2):
            h = blocks[2 * step + twin][...]
            spot = jnp.bitwise_xor(ids[CORE], twin)
            first = pl.multiple_of(
                (jnp.bitwise_xor(ids[PLANE], step) * 2 + spot) * rows, rows)
            span = pl.ds(first, rows)
            cosine, sine = cos_ref[span, :], sin_ref[span, :]
            dkv = dkv_ref[span, :]
            dqr, add_q = undo(dot_nn(h, wq), dq_ref[span, :], qg_ref[...], cosine, sine)
            dkr, add_k = undo(
                dot_nn(h, wkv), jnp.where(lanes < 64, dkv, 0.0), kg_ref[...], cosine, sine)
            q_gain = q_gain + add_q
            k_gain = k_gain + add_k
            dqr = dqr.astype(BF16)
            dkr = jnp.where(lanes < 64, dkr, dkv).astype(BF16)
            place = pl.ds(pl.multiple_of(spot * rows, rows), rows)
            backs[step][place, 0:LANES] = dqr
            backs[step][place, LANES:] = dkr
            for at, grad in ((slice(0, LANES), dqr), (slice(LANES, 2 * LANES), dkr)):
                term = dot_tn(grad, h)
                total[at, :] = term if step + twin == 0 else total[at, :] + term
    gains_ref[...] = jnp.concatenate([q_gain, k_gain, jnp.zeros((6, LANES), F32)], axis=0)
    for at, weight in ((slice(0, LANES), wq), (slice(LANES, 2 * LANES), wkv)):
        grad_ref[:, at] = jnp.transpose(total[at, :]).astype(BF16)
    row_ref[...] = jnp.sum(
        jnp.transpose(wq.astype(F32)) * total[0:LANES, :]
        + jnp.transpose(wkv.astype(F32)) * total[LANES:, :], axis=0, keepdims=True)


def unturn(ids, blocks, w_query, w_key, w_value, cosine, sine, qg, kg, dq, dkv, head_size, heads):
    rows, width = blocks[0].shape
    count = len(blocks) // 2
    head = lambda ids: ids[CORE] * heads + ids[PLANE]
    pair = pl.BlockSpec((width, LANES), lambda i, ids: (0, head(ids) // 2))
    row = whole((1, LANES))
    outs = [shaped(2 * rows, 2 * LANES)] * count + [
        shaped(width, 2 * LANES), shaped(1, width, dtype=F32), shaped(8, LANES, dtype=F32)]
    return run_kernel(
        functools.partial(unturn_kernel, head_size), "unturn", ids,
        (*blocks, w_query, w_key, w_value, cosine, sine, qg, kg, dq, dkv),
        [whole((rows, width))] * (2 * count)
        + [pl.BlockSpec((width, LANES), lambda i, ids: (0, head(ids))), pair, pair,
           whole(cosine.shape), whole(sine.shape), row, row, whole(dq.shape), whole(dkv.shape)],
        outs, [whole(o.shape) for o in outs],
        scratch=[pltpu.VMEM((2 * LANES, width), F32)], vmem=58, micros=7)


def back_kernel(ids, *refs):
    arrived, (wq_ref, wk_ref, wv_ref, own_ref, other_ref) = refs[:-5], refs[-5:]
    rows, width = own_ref.shape
    total = [jnp.zeros((rows, width), F32)] * 2
    for step in range(len(arrived)):
        head = jnp.bitwise_xor(ids[PLANE], step)
        span = pl.ds(pl.multiple_of(head * LANES, LANES), LANES)
        both = pl.ds(pl.multiple_of(head // 2 * LANES, LANES), LANES)
        wkv = pair_of(wk_ref[:, both].astype(F32), wv_ref[:, both].astype(F32), (head & 1) == 1,
                      lane_ids(width)).astype(BF16)
        wq = wq_ref[:, span]
        for twin in range(2):
            spot = jnp.bitwise_xor(ids[CORE], twin)
            grads = arrived[step][pl.ds(pl.multiple_of(spot * rows, rows), rows), :]
            total[twin] = total[twin] + dot_nt(grads[:, :LANES], wq) + dot_nt(grads[:, LANES:], wkv)
    own_ref[...] = total[0].astype(BF16)
    other_ref[...] = total[1].astype(BF16)


def to_tokens(ids, arrived, w_query, w_key, w_value):
    width = w_query.shape[0]
    rows = arrived[0].shape[0] // 2
    return run_kernel(
        back_kernel, "to_tokens", ids, (*arrived, w_query, w_key, w_value),
        [whole(a.shape) for a in arrived]
        + [of_core(width, w.shape[1] // 2) for w in (w_query, w_key, w_value)],
        [shaped(rows, width)] * 2, [whole((rows, width))] * 2, vmem=58, micros=4)


def last_kernel(ids, mine_ref, twin_ref, x_ref, dy_ref, gain_ref, out_ref):
    x = x_ref[...].astype(F32)
    scaled = (mine_ref[...].astype(F32) + twin_ref[...].astype(F32)) * gain_ref[...]
    scale = lax.rsqrt(jnp.mean(x * x, axis=1, keepdims=True) + EPSILON)
    unit = x * scale
    inner = jnp.mean(scaled * unit, axis=1, keepdims=True)
    out_ref[...] = dy_ref[...] + scale * (scaled - unit * inner)


def last(ids, mine, twin, x, dy, gain):
    part = whole(x.shape)
    return run_kernel(
        last_kernel, "last", ids, (mine, twin, x, dy, gain), [part] * 4 + [whole(gain.shape)],
        shaped(*x.shape, dtype=F32), part, vmem=24, micros=2)


def unpack_kernel(half, ids, kept_ref, got_ref, out_ref, q_ref, k_ref, v_ref):
    kept, got = kept_ref[...].astype(F32), got_ref[...].astype(F32)
    lanes = lane_ids(kept.shape[0])
    count = (kept.shape[1] - half) // (2 * LANES)
    odd = (ids[PLANE] & 1) == 1
    for core in range(2):
        rows = jnp.where(ids[CORE] == core, kept, got)
        out_ref[:, core * half : (core + 1) * half] = rows[:, :half]
        blocks = [rows[:, half + s * 2 * LANES :][:, : 2 * LANES] for s in range(count)]
        for s in range(count):
            head = core * count + jnp.bitwise_xor(ids[PLANE], s)
            q_ref[:, pl.ds(pl.multiple_of(head * LANES, LANES), LANES)] = blocks[s][:, :LANES]
        for s in range(0, count, 2):
            low = jnp.where(odd, blocks[s + 1][:, LANES:], blocks[s][:, LANES:])
            high = jnp.where(odd, blocks[s][:, LANES:], blocks[s + 1][:, LANES:])
            pair = core * (count // 2) + jnp.bitwise_xor(ids[PLANE], s) // 2
            span = pl.ds(pl.multiple_of(pair * LANES, LANES), LANES)
            k_ref[:, span] = jnp.where(lanes < 64, low, pltpu.roll(high, 64, 1))
            v_ref[:, span] = jnp.where(lanes < 64, pltpu.roll(low, 64, 1), high)


def unpack(ids, kept, got, half):
    rows = kept.shape[0]
    count = (kept.shape[1] - half) // (2 * LANES)
    outs = [shaped(rows, n, dtype=F32)
            for n in (2 * half, 2 * count * LANES, count * LANES, count * LANES)]
    return run_kernel(
        functools.partial(unpack_kernel, half), "unpack", ids, (kept, got),
        [whole(kept.shape), whole(got.shape)], outs, [whole(o.shape) for o in outs], vmem=16,
        micros=1)


def body(tokens, lengths, attn_gain, w_query, w_key, w_value, query_gain, key_gain, w_out,
         ffn_gain, w_gate, w_up, w_down, cotangent):
    rows, width = tokens.shape
    head_size = query_gain.shape[0]
    n_y, n_z = lax.axis_size("y"), lax.axis_size("z")
    i_y, i_x, i_z, i_c = (lax.axis_index(name) for name in ALL)
    heads = w_key.shape[1] // head_size // 2
    slots = lengths.shape[1]
    ids = jnp.concatenate(
        [jnp.stack([i_c, i_z, i_x, i_y]).astype(jnp.int32), lengths[0].astype(jnp.int32)])
    lane = np.arange(LANES)
    freq = jnp.asarray(
        (ROPE_BASE ** (-2.0 * (lane % (head_size // 2)) / head_size)).astype(np.float32))[None, :]
    to_exp2 = math.log2(math.e) / math.sqrt(head_size)
    qg = jnp.tile(query_gain, 2)[None, :]
    kg = jnp.tile(key_gain, 2)[None, :]
    a_gain, f_gain = attn_gain[None, :], ffn_gain[None, :]
    steps = range(1, n_z)

    x_other = swap(tokens, "c")
    h_own, h_other, *packed = project(
        ids, tokens, x_other, a_gain, w_query, w_key, w_value, freq, qg * to_exp2, kg, head_size,
        slots, heads)
    arrived = [packed[0]] + [crossed(packed[s], s, n_z) for s in steps]

    lengths_late = after(lengths, arrived[1])
    units = w_gate.shape[1] // 4
    token = jnp.arange(2 * rows * n_z, dtype=jnp.int32)
    start, edge = jnp.zeros_like(token), jnp.zeros((), jnp.int32)
    for slot in range(slots - 1):
        edge = edge + lengths_late[0, slot]
        start = jnp.where(token >= edge, edge, start)
    angles = (token - start).astype(F32)[:, None] * freq
    sign = jnp.asarray(np.where(lane % head_size < head_size // 2, -1.0, 1.0).astype(np.float32))
    cosine, sine = jnp.cos(angles), jnp.sin(angles) * sign[None, :]

    arrived = after(arrived, cosine, sine)
    *o_sent, wide, qaug, kaug, vaug = attend(ids, arrived, slots)
    o_own = [o_sent[0]] + [crossed(o_sent[s], s, n_z) for s in steps]
    o_other = [swap(o, "c") for o in [o_own[0]] + after(o_own[1:], *o_own[1:])]
    cot = after(cotangent, *o_own[1:])
    cot_other = swap(cot, "c")
    cot_far = swap(cot, "x")
    cot_far_other = swap(cot_far, "c")
    y_mine, h2_own, h2_other, o_rows = middle(
        ids, o_own, o_other, tokens, x_other, w_out, f_gain)

    h_line = after(h_own, h2_own)
    line = [along(h_line, h_line, n_z)]

    h2_far = swap(h2_own, "x")
    *kept, d_own, d_other, y_own, y_other = feed(
        ids, h2_own, h2_other, cot, cot_other, w_gate, w_up, w_down, (), units)
    h2_far_other = swap(after(h2_far, d_own, line[0]), "c")
    line.append(along(*line[0], n_z))
    d_twin = swap(d_other, "c")
    *kept, d_far, d_far_other, y_far, y_far_other = feed(
        ids, h2_far, after(h2_far_other, d_twin, cot_far_other), cot_far, cot_far_other, w_gate, w_up, w_down,
        tuple(kept), units)

    m, dg, du, h2_all, cot_all = kept
    piece = units // (n_y * n_z)
    row_block = width // (n_y * 2 * n_z * 2)
    grad_down = dot_tn(m, cot_all).astype(BF16)
    down = Pair(jnp.moveaxis(grad_down.reshape(n_z, n_y, piece, width), 1, 0), i_y)
    d_far_other, y_far, y_far_other, y_other = after(
        (d_far_other, y_far, y_far_other, y_other), line[1], down.sent)
    line.append(along(*line[1], n_z))
    d_sum = d_far + swap(d_far_other, "c")
    d_home = swap(d_sum, "x")
    y_far = y_far + swap(y_far_other, "c")
    y_near = y_own.astype(F32) + swap(y_other, "c").astype(F32)
    dg = after(dg, d_sum, y_far, y_near)
    grad_gate = dot_tn(h2_all, dg).astype(BF16).reshape(n_y, 2, n_z, 2, row_block, units)
    du = after(du, grad_gate)
    grad_up = dot_tn(h2_all, du).astype(BF16).reshape(n_y, 2, n_z, 2, row_block, units)
    d_home = after(d_home, grad_down, grad_gate, grad_up, *line[2])
    dy, da, gain_ffn = turn(ids, d_own, d_twin, d_home, y_mine, cotangent, f_gain)
    da_other = swap(da, "c")
    gate = Pair(grad_gate, i_y)
    y_home = swap(after(y_far, da), "x")
    da_cols, *do_sent = to_heads(ids, da, da_other, w_out, heads)
    do_sent = after(do_sent, down.got)
    near = jnp.where(i_z % 2 == 0, line[0][1], line[0][0])
    beyond = jnp.where(i_z <= 1, line[1][1], line[1][0])
    across = jnp.where(
        i_z == 0, line[2][1],
        jnp.where(i_z == 1, line[0][1], jnp.where(i_z == 2, line[0][0], line[2][0])))
    blocks = [h_own, h_other]
    for one in after((near, beyond, across), do_sent[0]):
        blocks += [one, swap(one, "c")]

    do_arrived = [do_sent[0]] + [crossed(do_sent[s], s, n_z) for s in steps]
    down = Halving(down.finish(*do_arrived[1:]), i_z)
    down.advance()
    out_parts = dot_tn(o_rows, after(da_cols, do_sent[0])).astype(BF16).reshape(
        n_y, 2, n_z, 2, row_block, width // 2)
    out_parts = Pair(jnp.moveaxis(out_parts, 1, 0), i_x, do_arrived[-1], axis_name="x")
    up = Pair(grad_up, i_y, do_sent[0])
    dq, dkv = attend_back(
        ids, qaug, kaug, vaug, wide, after(do_arrived, *blocks[3::2]))
    mixed = (y_mine + (y_near + after(y_home, dq).astype(F32))).astype(BF16)

    out_parts = out_parts.finish(dq)
    gate = Halving(jnp.moveaxis(gate.finish(dq), 1, 0), i_z)
    down.advance(dq)
    gate.advance()
    *back, grad_head, gain_attn, gains = unturn(
        ids, blocks, w_query, w_key, w_value, cosine, sine, qg, kg,
        after(dq, down.sent, gate.sent, out_parts, mixed), dkv, head_size, heads)
    up = Halving(jnp.moveaxis(up.finish(back[0]), 1, 0), i_z)
    back = after(back, down.parts, gate.parts, up.parts)
    back_arrived = [back[0]] + [crossed(back[s], s, n_z) for s in steps]
    late = tuple(back_arrived[1:])
    up.advance()
    dh_own, dh_other = to_tokens(ids, back_arrived, w_query, w_key, w_value)
    gate.advance(back_arrived[1])
    grad_tokens = last(ids, dh_own, swap(dh_other, "c"), tokens, dy, a_gain)

    owners = []
    for y in range(n_y):
        for x in range(2):
            for z in range(n_z):
                for c in range(2):
                    source = ((y * 2 + x) * n_z + z) * 2 + c
                    owners.append((source, n_y * n_z * (2 * x + c) + z * n_y + y))
    share_down = lax.ppermute(after(down.finish(), *late), ALL, owners).astype(F32)

    def spread(parts):
        got = swap(pick(parts, 1 - i_c, 1), "c")
        cols = in_order(i_c, pick(parts, i_c, 1), got, 2)
        got = swap(pick(cols, 1 - i_x), "x")
        return in_order(i_x, pick(cols, i_x), got, 1).astype(F32)

    share_gate = spread(gate.finish())
    share_up = spread(up.finish())

    half = width // 2
    sums = jnp.concatenate(
        [gain_attn / a_gain, gain_ffn, gains[0:1, :head_size] + gains[0:1, head_size:],
         gains[1:2, :head_size]], axis=1)
    total = sums.shape[1]
    sums = jnp.pad(sums, ((0, 0), (0, -total % (16 * 2 * LANES)))).reshape(-1, 2 * LANES)
    depth = sums.shape[0]
    parts = after(grad_head, back[0]).reshape(n_y, 2, n_z * 2 * row_block, 2 * LANES)
    parts = jnp.moveaxis(parts, 1, 0).reshape(2, -1, 2 * LANES)
    kept_x = pick(parts, i_x)
    got = swap(jnp.concatenate([pick(parts, 1 - i_x), *split_up(sums)], axis=0), "x")
    count = kept_x.shape[0]
    sums = sums + sum(got[count + k * depth :][:depth].astype(F32) for k in range(3))
    parts = jnp.concatenate([out_parts.reshape(-1, half), kept_x + got[:count]], axis=1)
    parts = parts.reshape(n_y, n_z * 2 * row_block, half + 2 * LANES)

    def joined(rows_sent, vector):
        beside = jnp.concatenate(split_up(vector), axis=1)
        wider = rows_sent.shape[1] - beside.shape[1]
        return jnp.concatenate([rows_sent, jnp.pad(beside, ((0, 0), (0, wider)))], axis=0)

    def parted(got):
        vector = got[-depth:].astype(F32)
        return got[:-depth], sum(
            vector[:, k * 2 * LANES : (k + 1) * 2 * LANES] for k in range(3))

    if n_y == 2:
        got, more = parted(swap(joined(pick(parts, 1 - i_y), sums), "y"))
        parts, sums = pick(parts, i_y) + got, sums + more
    else:
        parts = lax.psum_scatter(parts, "y", scatter_dimension=0, tiled=False)
        sums = lax.psum(sums, "y")
    parts = parts.reshape(n_z, 2 * row_block, half + 2 * LANES)
    kept_z, sums_z = pick(parts, i_z), sums
    out_sum, by_step = kept_z[:, :half].astype(F32), [kept_z[:, half:]]
    for s in steps:
        got, more = parted(crossed(joined(pick(parts, i_z ^ s), sums), s, n_z))
        out_sum, sums_z = out_sum + got[:, :half].astype(F32), sums_z + more
        by_step.append(got[:, half:])
    merged = jnp.concatenate([out_sum.astype(BF16), *by_step], axis=1)
    merged = merged.reshape(2, row_block, merged.shape[1])
    got, more = parted(swap(joined(pick(merged, 1 - i_c), sums_z), "c"))
    sums = (sums_z + more).reshape(-1)
    share_out, share_query, share_key, share_value = unpack(ids, pick(merged, i_c), got, half)

    return (
        mixed,
        grad_tokens,
        sums[:width],
        share_query,
        share_key,
        share_value,
        sums[2 * width : 2 * width + head_size],
        sums[2 * width + head_size : total],
        share_out,
        sums[width : 2 * width],
        share_gate,
        share_up,
        share_down,
    )


def solution(mesh):
    n_dp, n_seq = mesh.shape["dp"], mesh.shape["seq"]
    fine = Mesh(mesh.devices.reshape(n_dp // 2, 2, n_seq // 2, 2), ALL)
    split = P(ALL, None)
    in_specs = (split, P(("y", "x"), None)) + (P(),) * 11 + (split,)
    out_specs = (split, split, P(), split, split, split, P(), P(), split, P(), split, split, split)
    return jax.shard_map(body, mesh=fine, in_specs=in_specs, out_specs=out_specs, check_vma=False)
```

```python
import functools
import math

import jax
import jax.numpy as jnp
import numpy as np
from jax import lax
from jax.experimental import pallas as pl
from jax.experimental.pallas import tpu as pltpu
from jax.sharding import Mesh
from jax.sharding import PartitionSpec as P

EPSILON = 1e-05
ROPE_BASE = 1000000.0
FAR = 16384.0
LANES = 128
MIB = 1024 * 1024
ALL = ("y", "x", "z", "c")
F32 = jnp.float32
BF16 = jnp.bfloat16
CORE, PLANE, FIRST_LENGTH = 0, 1, 4


def dot_nn(left, right):
    return lax.dot_general(left, right, (((1,), (0,)), ((), ())), preferred_element_type=F32)


def dot_nt(left, right):
    return lax.dot_general(left, right, (((1,), (1,)), ((), ())), preferred_element_type=F32)


def dot_tn(left, right):
    return lax.dot_general(left, right, (((0,), (0,)), ((), ())), preferred_element_type=F32)


def after(value, *needed):
    return lax.optimization_barrier((value, needed))[0]


def pick(field, index, axis=0):
    return lax.dynamic_index_in_dim(field, index, axis, keepdims=False)


def swap(field, axis_name):
    return lax.ppermute(field, axis_name, [(0, 1), (1, 0)])


def crossed(field, step, count):
    return lax.ppermute(field, "z", [(k, k ^ step) for k in range(count)])


def along(to_right, to_left, count):
    pairs = range(count - 1)
    return (lax.ppermute(to_right, "z", [(k, k + 1) for k in pairs]),
            lax.ppermute(to_left, "z", [(k + 1, k) for k in pairs]))


class Pair:
    def __init__(self, parts, index, *needed, axis_name="y"):
        self.parts, self.index, self.sent, self.got = parts, index, parts, None
        if parts.shape[0] == 2:
            self.sent = after(pick(parts, 1 - index), *needed)
            self.got = swap(self.sent, axis_name)

    def finish(self, *needed):
        if self.parts.shape[0] == 1:
            return self.parts[0]
        if self.got is None:
            return lax.psum_scatter(self.parts, "y", scatter_dimension=0, tiled=False)
        return pick(self.parts, self.index) + after(self.got, *needed)


class Halving:
    def __init__(self, parts, index):
        self.parts, self.index, self.step, self.count = parts, index, 1, parts.shape[0]

    def advance(self, *needed):
        far = self.parts.shape[0] // 2
        parts = self.parts.reshape(far, 2, *self.parts.shape[1:])
        bit = (self.index // self.step) % 2
        sent = pick(parts, 1 - bit, 1)
        kept = pick(parts, bit, 1)
        if needed:
            sent = after(sent, *needed)
        self.sent, self.kept = sent, kept
        self.got = crossed(sent, self.step, self.count)
        self.parts = kept + self.got
        self.step = self.step * 2

    def finish(self, *needed):
        while self.step < self.count:
            self.advance()
        return after(self.parts, *needed)[0] if needed else self.parts[0]


def in_order(index, own, other, axis):
    return jnp.concatenate(
        [jnp.where(index == 0, own, other), jnp.where(index == 0, other, own)], axis=axis)


def split_up(field):
    high = field.astype(BF16)
    rest = field - high.astype(F32)
    middle = rest.astype(BF16)
    return [high, middle, (rest - middle.astype(F32)).astype(BF16)]


def run_kernel(kernel, name, ids, operands, in_specs, out_shapes, out_specs, grid=(1,), scratch=(),
               vmem=32, micros=5, aliases=None):
    return pl.pallas_call(
        kernel,
        grid_spec=pltpu.PrefetchScalarGridSpec(
            num_scalar_prefetch=1, grid=grid, in_specs=in_specs, out_specs=out_specs,
            scratch_shapes=list(scratch)),
        out_shape=out_shapes,
        input_output_aliases=aliases or {},
        compiler_params=pltpu.CompilerParams(vmem_limit_bytes=vmem * MIB),
        cost_estimate=pl.CostEstimate(
            flops=int(micros * 1e5), bytes_accessed=1024, transcendentals=0),
        name=name,
    )(ids, *operands)


def whole(shape):
    return pl.BlockSpec(tuple(shape), lambda i, ids: (0,) * len(shape))


def of_core(rows, cols):
    return pl.BlockSpec((rows, cols), lambda i, ids: (0, ids[CORE]))


IN_HBM = pl.BlockSpec(memory_space=pltpu.HBM)


def shaped(*shape, dtype=BF16):
    return jax.ShapeDtypeStruct(shape, dtype)


def lane_ids(rows):
    return lax.broadcasted_iota(jnp.int32, (rows, LANES), 1)


def half_swap(field, lanes):
    return jnp.where(
        (lanes & 63) < 32, pltpu.roll(field, LANES - 32, 1), pltpu.roll(field, 32, 1))


def low_sum(field, lanes):
    return jnp.sum(jnp.where(lanes < 64, field, 0.0), axis=1, keepdims=True)


def half_sums(field, lanes):
    high = jnp.sum(jnp.where(lanes < 64, 0.0, field), axis=1, keepdims=True)
    return jnp.where(lanes < 64, low_sum(field, lanes), high)


def twice(row):
    return jnp.concatenate([row, row], axis=1)


def tables(ids, slots, first_row, rows, freq):
    token = lax.broadcasted_iota(jnp.int32, (rows, LANES), 0) + first_row
    start = jnp.zeros((rows, LANES), jnp.int32)
    edge = jnp.int32(0)
    for slot in range(slots - 1):
        edge = edge + ids[FIRST_LENGTH + slot]
        start = jnp.where(token >= edge, edge, start)
    angles = (token - start).astype(F32) * freq
    sines = jnp.sin(angles)
    return jnp.cos(angles), jnp.where((lane_ids(rows) & 63) < 32, -sines, sines)


def project_kernel(head_size, slots, ids, xo_ref, xt_ref, gain_ref, wq_ref, wk_ref, wv_ref,
                   freq_ref, qg_ref, kg_ref, ho_ref, ht_ref, *refs):
    outs, packed = refs[:-1], refs[-1]
    heads, rows, _ = packed.shape
    turn = pl.program_id(0)
    x = jnp.where(turn == 0, xo_ref[...], xt_ref[...]).astype(F32)
    scale = lax.rsqrt(jnp.mean(x * x, axis=1, keepdims=True) + EPSILON)
    h = (x * scale * gain_ref[...]).astype(BF16)

    @pl.when(turn == 0)
    def _():
        ho_ref[...] = h

    @pl.when(turn == 1)
    def _():
        ht_ref[...] = h

    lanes = lane_ids(rows)
    spot = jnp.bitwise_xor(turn, ids[CORE])
    cosine, sine = tables(ids, slots, (ids[PLANE] * 2 + spot) * rows, rows, freq_ref[...])

    def turned(raw, gain):
        unit = raw * lax.rsqrt(half_sums(raw * raw, lanes) * (1.0 / head_size) + EPSILON) * gain
        return unit * cosine + half_swap(unit, lanes) * sine

    q_scale = twice(qg_ref[...]) * (math.log2(math.e) / math.sqrt(head_size))
    k_scale = twice(kg_ref[...])
    q_raw = dot_nn(h, wq_ref[...])
    k_raw = dot_nn(h, wk_ref[...])
    v_raw = dot_nn(h, wv_ref[...])
    for head in range(heads):
        span = slice(head * LANES, (head + 1) * LANES)
        packed[head, :, 0:LANES] = turned(q_raw[:, span], q_scale).astype(BF16)
    for pair in range(heads // 2):
        span = slice(pair * LANES, (pair + 1) * LANES)
        keys = turned(k_raw[:, span], k_scale)
        values = v_raw[:, span]
        even = jnp.where(lanes < 64, keys, pltpu.roll(values, 64, 1))
        odd = jnp.where(lanes < 64, pltpu.roll(keys, 64, 1), values)
        packed[2 * pair, :, LANES:] = even.astype(BF16)
        packed[2 * pair + 1, :, LANES:] = odd.astype(BF16)
    for step in range(heads):
        outs[step][...] = packed[jnp.bitwise_xor(ids[PLANE], step)]


def project(ids, x_own, x_other, gain, w_query, w_key, w_value, freq, qg, kg, head_size, slots,
            heads):
    rows, width = x_own.shape
    block = pl.BlockSpec((rows, 2 * LANES), lambda i, ids: (jnp.bitwise_xor(i, ids[CORE]), 0))
    part = whole((rows, width))
    row, gains = whole((1, LANES)), whole((1, head_size))
    return run_kernel(
        functools.partial(project_kernel, head_size, slots), "project", ids,
        (x_own, x_other, gain, w_query, w_key, w_value, freq, qg, kg),
        [part, part, whole((1, width)), of_core(width, w_query.shape[1] // 2),
         of_core(width, w_key.shape[1] // 2), of_core(width, w_value.shape[1] // 2), row, gains, gains],
        [shaped(rows, width)] * 2 + [shaped(2 * rows, 2 * LANES)] * heads,
        [part, part] + [block] * heads,
        grid=(2,), scratch=[pltpu.VMEM((heads, rows, 2 * LANES), BF16)], vmem=58,
        micros=5)


def three_parts(value):
    high = value.astype(BF16).astype(F32)
    rest = value - high
    middle = rest.astype(BF16).astype(F32)
    return high, middle, rest - middle


def marked(lanes, first, value, otherwise):
    high, middle, low = three_parts(value)
    return jnp.where(
        lanes == first, high,
        jnp.where(lanes == first + 1, middle, jnp.where(lanes == first + 2, low, otherwise)))


def below(rows, cols):
    return lax.broadcasted_iota(jnp.int32, (rows, cols), 1) <= lax.broadcasted_iota(
        jnp.int32, (rows, cols), 0)


def attend_kernel(slots, ids, *refs):
    count = (len(refs) - 6) // 2
    sources, sent = refs[:count], refs[count : 2 * count]
    wide_ref, qaug_ref, kaug_ref, vaug_ref, arrived, arrivals = refs[2 * count :]
    block = arrived.shape[1]
    copies = [pltpu.make_async_copy(source, arrived.at[k], arrivals.at[k])
              for k, source in enumerate(sources)]
    for copy in copies:
        copy.start()
    mark = 64 + slots
    lanes = lane_ids(block)
    plane = ids[PLANE]
    slot_lane = (lanes >= 64) & (lanes < mark)
    ones_lane = (lanes >= mark) & (lanes < mark + 3)
    for step in range(count):
        first = pl.multiple_of(jnp.bitwise_xor(plane, step) * block, block)
        span = pl.ds(first, block)
        token = lax.broadcasted_iota(jnp.int32, (block, LANES), 0) + first
        inside = lanes < 0
        edge = jnp.int32(0)
        for slot in range(slots):
            stop = edge + ids[FIRST_LENGTH + slot]
            inside = inside | ((lanes == 64 + slot) & (token >= edge) & (token < stop))
            edge = stop
        segq = jnp.where(inside, 1.0, 0.0)
        segk = jnp.where(ones_lane, 1.0, jnp.where(slot_lane & jnp.logical_not(inside), -FAR, 0.0))
        copies[step].wait()
        pair = arrived[step, :, 0:LANES].astype(F32)
        keyval = arrived[step, :, LANES:].astype(F32)
        qaug_ref[0, span, :] = jnp.where(lanes < 64, pair, segq).astype(BF16)
        qaug_ref[1, span, :] = jnp.where(lanes < 64, pltpu.roll(pair, 64, 1), segq).astype(BF16)
        kaug_ref[span, :] = jnp.where(lanes < 64, keyval, segk).astype(BF16)
        vaug_ref[span, :] = jnp.where(
            lanes < 64, pltpu.roll(keyval, 64, 1), jnp.where(lanes < 67, 1.0, 0.0)).astype(BF16)
    for i in range(count):
        span = slice(i * block, (i + 1) * block)
        outs = []
        for head in range(2):
            queries = qaug_ref[head, span, :]
            total = jnp.zeros((block, LANES), F32)
            for j in range(i + 1):
                other = slice(j * block, (j + 1) * block)
                weights = jnp.exp2(dot_nt(queries, kaug_ref[other, :]))
                if j == i:
                    weights = jnp.where(below(block, block), weights, 0.0)
                total = total + dot_nn(weights.astype(BF16), vaug_ref[other, :])
            row_sum = total[:, 64:65]
            outs.append(total * (1.0 / row_sum))
            qaug_ref[head, span, :] = marked(
                lanes, mark, -jnp.log2(row_sum), queries.astype(F32)).astype(BF16)
        wide_ref[span, :] = jnp.where(lanes < 64, outs[0], pltpu.roll(outs[1], 64, 1))
    for step in range(count):
        first = pl.multiple_of(jnp.bitwise_xor(plane, step) * block, block)
        sent[step][...] = wide_ref[pl.ds(first, block), :].astype(BF16)


def attend(ids, arrived, slots):
    count, block = len(arrived), arrived[0].shape[0]
    rows = count * block
    outs = [shaped(block, LANES)] * count + [
        shaped(rows, LANES, dtype=F32), shaped(2, rows, LANES), shaped(rows, LANES),
        shaped(rows, LANES)]
    return run_kernel(
        functools.partial(attend_kernel, slots), "attend", ids, arrived,
        [IN_HBM] * count, outs, [whole(o.shape) for o in outs],
        scratch=[pltpu.VMEM((count, block, 2 * LANES), BF16), pltpu.SemaphoreType.DMA((count,))],
        vmem=40,
        micros=9)


def middle_kernel(count, ids, *refs):
    blocks = refs[: 2 * count]
    xo_ref, xt_ref, w_ref, gain_ref, y_ref, ho_ref, ht_ref, o_ref, arrivals = refs[2 * count :]
    rows = xo_ref.shape[0]
    copies = []
    for twin in range(2):
        core = jnp.bitwise_xor(ids[CORE], twin)
        for step in range(count):
            head = core * count + jnp.bitwise_xor(ids[PLANE], step)
            span = pl.ds(pl.multiple_of(head * LANES, LANES), LANES)
            for half in range(2):
                spot = pl.multiple_of(jnp.bitwise_xor(ids[CORE], half) * rows, rows)
                copies.append(pltpu.make_async_copy(
                    blocks[twin * count + step].at[pl.ds(spot, rows), :],
                    o_ref.at[half * rows : (half + 1) * rows, span],
                    arrivals.at[len(copies)]))
                copies[-1].start()
    for copy in copies:
        copy.wait()
    for half, x_ref, h_ref in ((0, xo_ref, ho_ref), (1, xt_ref, ht_ref)):
        y = x_ref[...].astype(F32) + dot_nn(o_ref[half * rows : (half + 1) * rows, :], w_ref[...])
        if half == 0:
            y_ref[...] = y
        scale = lax.rsqrt(jnp.mean(y * y, axis=1, keepdims=True) + EPSILON)
        h_ref[...] = (y * scale * gain_ref[...]).astype(BF16)


def middle(ids, own, other, x_own, x_other, w_out, gain):
    rows, width = x_own.shape
    count = len(own)
    part = whole((rows, width))
    return run_kernel(
        functools.partial(middle_kernel, count), "middle", ids,
        (*own, *other, x_own, x_other, w_out, gain),
        [IN_HBM] * (2 * count) + [part, part, whole(w_out.shape), whole((1, width))],
        [shaped(rows, width, dtype=F32), shaped(rows, width), shaped(rows, width),
         shaped(2 * rows, width)],
        [part, part, part, whole((2 * rows, width))],
        scratch=[pltpu.SemaphoreType.DMA((4 * count,))], vmem=32, micros=4)


def feed_kernel(ids, ho_all, ht_all, co_all, ct_all, wg_all, wu_all, wd_all, *refs):
    m_ref, dg_ref, du_ref, ha_ref, ca_ref, do_ref, dt_ref, yo_ref, yt_ref = refs[-13:-4]
    wg_ref, wu_ref, wd_ref, arrivals = refs[-4:]
    rows = ho_all.shape[0]
    units = wg_ref.shape[1]
    mine = pl.ds(pl.multiple_of((2 * ids[2] + ids[CORE]) * units, LANES), units)
    gates = pltpu.make_async_copy(wg_all.at[:, mine], wg_ref, arrivals.at[0])
    ups = pltpu.make_async_copy(wu_all.at[:, mine], wu_ref, arrivals.at[1])
    downs = pltpu.make_async_copy(wd_all.at[mine, :], wd_ref, arrivals.at[2])
    blocks = [
        pltpu.make_async_copy(source, target.at[half * rows : (half + 1) * rows, :],
                              arrivals.at[3 + k])
        for k, (source, target, half) in enumerate((
            (ho_all, ha_ref, 0), (ht_all, ha_ref, 1), (co_all, ca_ref, 0), (ct_all, ca_ref, 1)))]
    for copy in (*blocks[:2], gates, ups, *blocks[2:], downs):
        copy.start()
    blocks[0].wait()
    blocks[1].wait()
    gates.wait()
    gate = dot_nn(ha_ref[...], wg_ref[...])
    ups.wait()
    up = dot_nn(ha_ref[...], wu_ref[...])
    blocks[2].wait()
    blocks[3].wait()
    downs.wait()
    sig = jax.nn.sigmoid(gate)
    silu = gate * sig
    m_ref[...] = (silu * up).astype(BF16)
    dm = dot_nt(ca_ref[...], wd_ref[...])
    dg_ref[...] = (dm * up * sig * (1.0 + gate * (1.0 - sig))).astype(BF16)
    du_ref[...] = (dm * silu).astype(BF16)
    dh = dot_nt(dg_ref[...], wg_ref[...]) + dot_nt(du_ref[...], wu_ref[...])
    do_ref[...] = dh[:rows].astype(BF16)
    dt_ref[...] = dh[rows:].astype(BF16)
    y = dot_nn(m_ref[...], wd_ref[...])
    yo_ref[...] = y[:rows].astype(BF16)
    yt_ref[...] = y[rows:].astype(BF16)


def feed(ids, h_own, h_other, c_own, c_other, w_gate, w_up, w_down, earlier, units):
    rows, width = h_own.shape
    half = 1 if earlier else 0
    part = whole((rows, width))
    anywhere = pl.BlockSpec(memory_space=pl.ANY)
    kept = lambda cols: pl.BlockSpec((2 * rows, cols), lambda i, ids: (half, 0))
    cols = [units] * 3 + [width] * 2
    return run_kernel(
        feed_kernel, "feed", ids, (h_own, h_other, c_own, c_other, w_gate, w_up, w_down, *earlier),
        [IN_HBM] * 4 + [anywhere] * (3 + len(earlier)),
        [shaped(4 * rows, n) for n in cols] + [shaped(rows, width)] * 4,
        [kept(n) for n in cols] + [part] * 4,
        scratch=[pltpu.VMEM((width, units), BF16)] * 2
        + [pltpu.VMEM((units, width), BF16), pltpu.SemaphoreType.DMA((7,))],
        vmem=58, micros=12, aliases={8 + k: k for k in range(len(earlier))})


def turn_kernel(ids, near_ref, twin_ref, far_ref, y_ref, c_ref, gain_ref, dy_ref, da_ref, sum_ref):
    y = y_ref[...]
    grad = near_ref[...].astype(F32) + twin_ref[...].astype(F32) + far_ref[...].astype(F32)
    scale = lax.rsqrt(jnp.mean(y * y, axis=1, keepdims=True) + EPSILON)
    unit = y * scale
    scaled = grad * gain_ref[...]
    inner = jnp.mean(scaled * unit, axis=1, keepdims=True)
    dy = c_ref[...].astype(F32) + scale * (scaled - unit * inner)
    dy_ref[...] = dy
    da_ref[...] = dy.astype(BF16)
    sum_ref[...] = jnp.sum(grad * unit, axis=0, keepdims=True)


def turn(ids, near, twin, far, y, c, gain):
    part, line = whole(y.shape), whole(gain.shape)
    return run_kernel(
        turn_kernel, "turn", ids, (near, twin, far, y, c, gain), [part] * 5 + [line],
        [shaped(*y.shape, dtype=F32), shaped(*y.shape), shaped(*gain.shape, dtype=F32)],
        [part, part, line], vmem=24, micros=2)


def heads_kernel(count, ids, ao_ref, at_ref, w_ref, cols_ref, *outs):
    a = jnp.where(pl.program_id(0) == 0, ao_ref[...], at_ref[...])
    half = cols_ref.shape[1]
    cols_ref[...] = jnp.where(ids[CORE] == 0, a[:, :half], a[:, half:])
    for step in range(count):
        head = ids[CORE] * count + jnp.bitwise_xor(ids[PLANE], step)
        span = pl.ds(pl.multiple_of(head * LANES, LANES), LANES)
        outs[step][...] = dot_nt(a, w_ref[span, :]).astype(BF16)


def to_heads(ids, da_own, da_other, w_out, count):
    rows, width = da_own.shape
    block = pl.BlockSpec((rows, LANES), lambda i, ids: (jnp.bitwise_xor(i, ids[CORE]), 0))
    part = whole((rows, width))
    return run_kernel(
        functools.partial(heads_kernel, count), "to_heads", ids, (da_own, da_other, w_out),
        [part, part, whole(w_out.shape)],
        [shaped(2 * rows, width // 2)] + [shaped(2 * rows, LANES)] * count,
        [pl.BlockSpec((rows, width // 2), lambda i, ids: (i, 0))] + [block] * count,
        grid=(2,), vmem=24, micros=2)


def attend_back_kernel(ids, qaug_ref, kaug_ref, vaug_ref, wide_ref, *refs):
    arrived, (dq_ref, dkv_ref, doaug, dq_sum) = refs[:-4], refs[-4:]
    count, block = len(arrived), arrived[0].shape[0]
    lanes = lane_ids(block)
    for step in range(count):
        first = pl.multiple_of(jnp.bitwise_xor(ids[PLANE], step) * block, block)
        span = pl.ds(first, block)
        do_pair = arrived[step][...].astype(F32)
        inner = do_pair * wide_ref[span, :]
        low = jnp.sum(jnp.where(lanes < 64, inner, 0.0), axis=1, keepdims=True)
        high = jnp.sum(jnp.where(lanes < 64, 0.0, inner), axis=1, keepdims=True)
        doaug[0, span, :] = jnp.where(
            lanes < 64, do_pair, marked(lanes, 64, -low, 0.0)).astype(BF16)
        doaug[1, span, :] = jnp.where(
            lanes < 64, pltpu.roll(do_pair, 64, 1), marked(lanes, 64, -high, 0.0)).astype(BF16)
    dq_sum[...] = jnp.zeros(dq_sum.shape, F32)
    for j in range(count):
        here = slice(j * block, (j + 1) * block)
        keys = kaug_ref[here, :]
        values = vaug_ref[here, :]
        dk = jnp.zeros((LANES, block), F32)
        dv = jnp.zeros((LANES, block), F32)
        for i in range(j, count):
            span = slice(i * block, (i + 1) * block)
            for head in range(2):
                queries = qaug_ref[head, span, :]
                grads = doaug[head, span, :]
                weights = jnp.exp2(dot_nt(queries, keys))
                if j == i:
                    weights = jnp.where(below(block, block), weights, 0.0)
                slopes = (weights * dot_nt(grads, values)).astype(BF16)
                dv = dv + dot_tn(grads, weights.astype(BF16))
                dk = dk + dot_tn(queries, slopes)
                dq_sum[head, span, :] = dq_sum[head, span, :] + dot_nn(slopes, keys)
        dk_rows = jnp.transpose(dk) * math.log(2.0)
        dv_rows = jnp.transpose(dv)
        dkv_ref[here, :] = jnp.where(lanes < 64, dk_rows, pltpu.roll(dv_rows, 64, 1))
    for i in range(count):
        span = slice(i * block, (i + 1) * block)
        dq_ref[span, :] = jnp.where(
            lanes < 64, dq_sum[0, span, :], pltpu.roll(dq_sum[1, span, :], 64, 1)) * 0.125


def attend_back(ids, qaug, kaug, vaug, wide, arrived):
    rows = kaug.shape[0]
    operands = (qaug, kaug, vaug, wide, *arrived)
    outs = [shaped(rows, LANES, dtype=F32)] * 2
    return run_kernel(
        attend_back_kernel, "attend_back", ids, operands, [whole(a.shape) for a in operands], outs,
        [whole(o.shape) for o in outs],
        scratch=[pltpu.VMEM((2, rows, LANES), BF16), pltpu.VMEM((2, rows, LANES), F32)], vmem=44,
        micros=13)


def pair_of(wk, wv, odd, lanes):
    keys = jnp.where(odd, pltpu.roll(wk, 64, 1), wk)
    values = jnp.where(odd, wv, pltpu.roll(wv, 64, 1))
    return jnp.where(lanes < 64, keys, values)


def unturn_kernel(head_size, ids, *refs):
    count = (len(refs) - 13) // 3
    blocks = refs[: 2 * count]
    wq_ref, wk_ref, wv_ref, cos_ref, sin_ref, qg_ref, kg_ref, dq_ref, dkv_ref = refs[
        2 * count : 2 * count + 9]
    backs = refs[2 * count + 9 : 3 * count + 9]
    grad_ref, row_ref, gains_ref, total = refs[3 * count + 9 :]
    rows = blocks[0].shape[0]
    width = wq_ref.shape[0]
    lanes = lane_ids(rows)
    odd = (ids[PLANE] & 1) == 1
    wkv = pair_of(
        wk_ref[...].astype(F32), wv_ref[...].astype(F32), odd, lane_ids(width)).astype(BF16)
    wq = wq_ref[...]

    def undo(raw, grad, gain, cosine, sine, sums):
        scale = lax.rsqrt(sums(raw * raw, lanes) * (1.0 / head_size) + EPSILON)
        unit = raw * scale
        back = grad * cosine - half_swap(grad, lanes) * sine
        scaled = back * gain
        mean = sums(scaled * unit, lanes) * (1.0 / head_size)
        return scale * (scaled - unit * mean), jnp.sum(back * unit, axis=0, keepdims=True)

    q_scale, k_scale = twice(qg_ref[...]), twice(kg_ref[...])
    q_gain = jnp.zeros((1, LANES), F32)
    k_gain = jnp.zeros((1, LANES), F32)
    for step in range(count):
        for twin in range(2):
            h = blocks[2 * step + twin][...]
            spot = jnp.bitwise_xor(ids[CORE], twin)
            first = pl.multiple_of(
                (jnp.bitwise_xor(ids[PLANE], step) * 2 + spot) * rows, rows)
            span = pl.ds(first, rows)
            cosine, sine = cos_ref[span, :], sin_ref[span, :]
            dkv = dkv_ref[span, :]
            dqr, add_q = undo(
                dot_nn(h, wq), dq_ref[span, :], q_scale, cosine, sine, half_sums)
            dkr, add_k = undo(
                dot_nn(h, wkv), jnp.where(lanes < 64, dkv, 0.0), k_scale, cosine, sine, low_sum)
            q_gain = q_gain + add_q
            k_gain = k_gain + add_k
            dqr = dqr.astype(BF16)
            dkr = jnp.where(lanes < 64, dkr, dkv).astype(BF16)
            place = pl.ds(pl.multiple_of(spot * rows, rows), rows)
            backs[step][place, 0:LANES] = dqr
            backs[step][place, LANES:] = dkr
            for at, grad in ((slice(0, LANES), dqr), (slice(LANES, 2 * LANES), dkr)):
                term = dot_tn(grad, h)
                total[at, :] = term if step + twin == 0 else total[at, :] + term
    gains_ref[...] = jnp.concatenate([q_gain, k_gain, jnp.zeros((6, LANES), F32)], axis=0)
    for at, weight in ((slice(0, LANES), wq), (slice(LANES, 2 * LANES), wkv)):
        grad_ref[:, at] = jnp.transpose(total[at, :]).astype(BF16)
    row_ref[...] = jnp.sum(
        jnp.transpose(wq.astype(F32)) * total[0:LANES, :]
        + jnp.transpose(wkv.astype(F32)) * total[LANES:, :], axis=0, keepdims=True)


def unturn(ids, blocks, w_query, w_key, w_value, cosine, sine, qg, kg, dq, dkv, head_size, heads):
    rows, width = blocks[0].shape
    count = len(blocks) // 2
    head = lambda ids: ids[CORE] * heads + ids[PLANE]
    pair = pl.BlockSpec((width, LANES), lambda i, ids: (0, head(ids) // 2))
    row = whole((1, head_size))
    outs = [shaped(2 * rows, 2 * LANES)] * count + [
        shaped(width, 2 * LANES), shaped(1, width, dtype=F32), shaped(8, LANES, dtype=F32)]
    return run_kernel(
        functools.partial(unturn_kernel, head_size), "unturn", ids,
        (*blocks, w_query, w_key, w_value, cosine, sine, qg, kg, dq, dkv),
        [whole((rows, width))] * (2 * count)
        + [pl.BlockSpec((width, LANES), lambda i, ids: (0, head(ids))), pair, pair,
           whole(cosine.shape), whole(sine.shape), row, row, whole(dq.shape), whole(dkv.shape)],
        outs, [whole(o.shape) for o in outs],
        scratch=[pltpu.VMEM((2 * LANES, width), F32)], vmem=40, micros=7)


def back_kernel(ids, *refs):
    arrived, (wq_ref, wk_ref, wv_ref, own_ref, other_ref) = refs[:-5], refs[-5:]
    rows, width = own_ref.shape
    total = [jnp.zeros((rows, width), F32)] * 2
    for step in range(len(arrived)):
        head = jnp.bitwise_xor(ids[PLANE], step)
        span = pl.ds(pl.multiple_of(head * LANES, LANES), LANES)
        both = pl.ds(pl.multiple_of(head // 2 * LANES, LANES), LANES)
        wkv = pair_of(wk_ref[:, both].astype(F32), wv_ref[:, both].astype(F32), (head & 1) == 1,
                      lane_ids(width)).astype(BF16)
        wq = wq_ref[:, span]
        for twin in range(2):
            spot = jnp.bitwise_xor(ids[CORE], twin)
            grads = arrived[step][pl.ds(pl.multiple_of(spot * rows, rows), rows), :]
            total[twin] = total[twin] + dot_nt(grads[:, :LANES], wq) + dot_nt(grads[:, LANES:], wkv)
    own_ref[...] = total[0].astype(BF16)
    other_ref[...] = total[1].astype(BF16)


def to_tokens(ids, arrived, w_query, w_key, w_value):
    width = w_query.shape[0]
    rows = arrived[0].shape[0] // 2
    return run_kernel(
        back_kernel, "to_tokens", ids, (*arrived, w_query, w_key, w_value),
        [whole(a.shape) for a in arrived]
        + [of_core(width, w.shape[1] // 2) for w in (w_query, w_key, w_value)],
        [shaped(rows, width)] * 2, [whole((rows, width))] * 2, vmem=24, micros=4)


def last_kernel(ids, mine_ref, twin_ref, x_ref, dy_ref, gain_ref, out_ref):
    x = x_ref[...].astype(F32)
    scaled = (mine_ref[...].astype(F32) + twin_ref[...].astype(F32)) * gain_ref[...]
    scale = lax.rsqrt(jnp.mean(x * x, axis=1, keepdims=True) + EPSILON)
    unit = x * scale
    inner = jnp.mean(scaled * unit, axis=1, keepdims=True)
    out_ref[...] = dy_ref[...] + scale * (scaled - unit * inner)


def last(ids, mine, twin, x, dy, gain):
    part = whole(x.shape)
    return run_kernel(
        last_kernel, "last", ids, (mine, twin, x, dy, gain), [part] * 4 + [whole(gain.shape)],
        shaped(*x.shape, dtype=F32), part, vmem=24, micros=2)


def unpack_kernel(half, ids, kept_ref, got_ref, out_ref, q_ref, k_ref, v_ref):
    kept, got = kept_ref[...].astype(F32), got_ref[...].astype(F32)
    lanes = lane_ids(kept.shape[0])
    count = (kept.shape[1] - half) // (2 * LANES)
    odd = (ids[PLANE] & 1) == 1
    for core in range(2):
        rows = jnp.where(ids[CORE] == core, kept, got)
        out_ref[:, core * half : (core + 1) * half] = rows[:, :half]
        blocks = [rows[:, half + s * 2 * LANES :][:, : 2 * LANES] for s in range(count)]
        for s in range(count):
            head = core * count + jnp.bitwise_xor(ids[PLANE], s)
            q_ref[:, pl.ds(pl.multiple_of(head * LANES, LANES), LANES)] = blocks[s][:, :LANES]
        for s in range(0, count, 2):
            low = jnp.where(odd, blocks[s + 1][:, LANES:], blocks[s][:, LANES:])
            high = jnp.where(odd, blocks[s][:, LANES:], blocks[s + 1][:, LANES:])
            pair = core * (count // 2) + jnp.bitwise_xor(ids[PLANE], s) // 2
            span = pl.ds(pl.multiple_of(pair * LANES, LANES), LANES)
            k_ref[:, span] = jnp.where(lanes < 64, low, pltpu.roll(high, 64, 1))
            v_ref[:, span] = jnp.where(lanes < 64, pltpu.roll(low, 64, 1), high)


def unpack(ids, kept, got, half):
    rows = kept.shape[0]
    count = (kept.shape[1] - half) // (2 * LANES)
    outs = [shaped(rows, n, dtype=F32)
            for n in (2 * half, 2 * count * LANES, count * LANES, count * LANES)]
    return run_kernel(
        functools.partial(unpack_kernel, half), "unpack", ids, (kept, got),
        [whole(kept.shape), whole(got.shape)], outs, [whole(o.shape) for o in outs], vmem=16,
        micros=1)


def body(tokens, lengths, attn_gain, w_query, w_key, w_value, query_gain, key_gain, w_out,
         ffn_gain, w_gate, w_up, w_down, cotangent):
    rows, width = tokens.shape
    head_size = query_gain.shape[0]
    n_y, n_z = lax.axis_size("y"), lax.axis_size("z")
    i_y, i_x, i_z, i_c = (lax.axis_index(name) for name in ALL)
    heads = w_key.shape[1] // head_size // 2
    slots = lengths.shape[1]
    ids = jnp.concatenate(
        [jnp.stack([i_c, i_z, i_x, i_y]).astype(jnp.int32), lengths[0].astype(jnp.int32)])
    lane = np.arange(LANES)
    freq = jnp.asarray(
        (ROPE_BASE ** (-2.0 * (lane % (head_size // 2)) / head_size)).astype(np.float32))[None, :]
    qg, kg = query_gain[None, :], key_gain[None, :]
    a_gain, f_gain = attn_gain[None, :], ffn_gain[None, :]
    steps = range(1, n_z)

    x_other = swap(tokens, "c")
    h_own, h_other, *packed = project(
        ids, tokens, x_other, a_gain, w_query, w_key, w_value, freq, qg, kg, head_size,
        slots, heads)
    arrived = [packed[0]] + [crossed(packed[s], s, n_z) for s in steps]

    lengths_late = after(lengths, arrived[1])
    units = w_gate.shape[1] // 4
    token = jnp.arange(2 * rows * n_z, dtype=jnp.int32)
    start, edge = jnp.zeros_like(token), jnp.zeros((), jnp.int32)
    for slot in range(slots - 1):
        edge = edge + lengths_late[0, slot]
        start = jnp.where(token >= edge, edge, start)
    angles = (token - start).astype(F32)[:, None] * freq
    sign = jnp.asarray(np.where(lane % head_size < head_size // 2, -1.0, 1.0).astype(np.float32))
    cosine, sine = jnp.cos(angles), jnp.sin(angles) * sign[None, :]

    arrived = after(arrived, cosine, sine)
    *o_sent, wide, qaug, kaug, vaug = attend(ids, arrived, slots)
    o_own = [o_sent[0]] + [crossed(o_sent[s], s, n_z) for s in steps]
    o_other = [swap(o, "c") for o in [o_own[0]] + after(o_own[1:], *o_own[1:])]
    cot = after(cotangent, *o_own[1:])
    cot_other = swap(cot, "c")
    cot_far = swap(cot, "x")
    cot_far_other = swap(cot_far, "c")
    y_mine, h2_own, h2_other, o_rows = middle(
        ids, o_own, o_other, tokens, x_other, w_out, f_gain)

    h_line = after(h_own, h2_own)
    line = [along(h_line, h_line, n_z)]

    h2_far = swap(h2_own, "x")
    *kept, d_own, d_other, y_own, y_other = feed(
        ids, h2_own, h2_other, cot, cot_other, w_gate, w_up, w_down, (), units)
    h2_far_other = swap(after(h2_far, d_own, line[0]), "c")
    line.append(along(*line[0], n_z))
    d_twin = swap(d_other, "c")
    *kept, d_far, d_far_other, y_far, y_far_other = feed(
        ids, h2_far, after(h2_far_other, d_twin, cot_far_other), cot_far, cot_far_other, w_gate, w_up, w_down,
        tuple(kept), units)

    m, dg, du, h2_all, cot_all = kept
    piece = units // (n_y * n_z)
    row_block = width // (n_y * 2 * n_z * 2)
    grad_down = dot_tn(m, cot_all).astype(BF16)
    down = Pair(jnp.moveaxis(grad_down.reshape(n_z, n_y, piece, width), 1, 0), i_y)
    d_far_other, y_far, y_far_other, y_other = after(
        (d_far_other, y_far, y_far_other, y_other), line[1], down.sent)
    line.append(along(*line[1], n_z))
    d_sum = d_far + swap(d_far_other, "c")
    d_home = swap(d_sum, "x")
    y_far = y_far + swap(y_far_other, "c")
    y_near = y_own.astype(F32) + swap(y_other, "c").astype(F32)
    dg = after(dg, d_sum, y_far, y_near)
    grad_gate = dot_tn(h2_all, dg).astype(BF16).reshape(n_y, 2, n_z, 2, row_block, units)
    du = after(du, grad_gate)
    grad_up = dot_tn(h2_all, du).astype(BF16).reshape(n_y, 2, n_z, 2, row_block, units)
    d_home = after(d_home, grad_down, grad_gate, grad_up, *line[2])
    dy, da, gain_ffn = turn(ids, d_own, d_twin, d_home, y_mine, cotangent, f_gain)
    da_other = swap(da, "c")
    gate = Pair(grad_gate, i_y)
    y_home = swap(after(y_far, da), "x")
    da_cols, *do_sent = to_heads(ids, da, da_other, w_out, heads)
    do_sent = after(do_sent, down.got)
    near = jnp.where(i_z % 2 == 0, line[0][1], line[0][0])
    beyond = jnp.where(i_z <= 1, line[1][1], line[1][0])
    across = jnp.where(
        i_z == 0, line[2][1],
        jnp.where(i_z == 1, line[0][1], jnp.where(i_z == 2, line[0][0], line[2][0])))
    blocks = [h_own, h_other]
    for one in after((near, beyond, across), do_sent[0]):
        blocks += [one, swap(one, "c")]

    do_arrived = [do_sent[0]] + [crossed(do_sent[s], s, n_z) for s in steps]
    down = Halving(down.finish(*do_arrived[1:]), i_z)
    down.advance()
    out_parts = dot_tn(o_rows, after(da_cols, do_sent[0])).astype(BF16).reshape(
        n_y, 2, n_z, 2, row_block, width // 2)
    out_parts = Pair(jnp.moveaxis(out_parts, 1, 0), i_x, do_arrived[-1], axis_name="x")
    up = Pair(grad_up, i_y, do_sent[0])
    dq, dkv = attend_back(
        ids, qaug, kaug, vaug, wide, after(do_arrived, *blocks[3::2]))
    mixed = (y_mine + (y_near + after(y_home, dq).astype(F32))).astype(BF16)

    gate = Halving(jnp.moveaxis(gate.finish(dq), 1, 0), i_z)
    down.advance(dq)
    gate.advance()
    *back, grad_head, gain_attn, gains = unturn(
        ids, blocks, w_query, w_key, w_value, cosine, sine, qg, kg,
        after(dq, down.sent, gate.sent, mixed), dkv, head_size, heads)
    up = Halving(jnp.moveaxis(up.finish(back[0]), 1, 0), i_z)
    back = after(back, down.parts, gate.parts, up.parts)
    back_arrived = [back[0]] + [crossed(back[s], s, n_z) for s in steps]
    late = tuple(back_arrived[1:])
    gain_attn, gains = after((gain_attn, gains), back_arrived[1])
    up.advance()
    half = width // 2
    sums = jnp.concatenate(
        [gain_attn / a_gain, gain_ffn, gains[0:1, :head_size] + gains[0:1, head_size:],
         gains[1:2, :head_size]], axis=1)
    total = sums.shape[1]
    sums = jnp.pad(sums, ((0, 0), (0, -total % (16 * 2 * LANES)))).reshape(-1, 2 * LANES)
    depth = sums.shape[0]
    parts = after(grad_head, back[0]).reshape(n_y, 2, n_z * 2 * row_block, 2 * LANES)
    parts = jnp.moveaxis(parts, 1, 0).reshape(2, -1, 2 * LANES)
    kept_x = pick(parts, i_x)
    got = swap(jnp.concatenate([pick(parts, 1 - i_x), *split_up(sums)], axis=0), "x")
    count = kept_x.shape[0]
    sums = sums + sum(got[count + k * depth :][:depth].astype(F32) for k in range(3))
    parts = jnp.concatenate(
        [out_parts.finish(back[0]).reshape(-1, half), kept_x + got[:count]], axis=1)
    parts = parts.reshape(n_y, n_z * 2 * row_block, half + 2 * LANES)

    dh_own, dh_other = to_tokens(ids, after(back_arrived, parts), w_query, w_key, w_value)
    gate.advance(back_arrived[1])
    def joined(rows_sent, vector):
        beside = jnp.concatenate(split_up(vector), axis=1)
        wider = rows_sent.shape[1] - beside.shape[1]
        return jnp.concatenate([rows_sent, jnp.pad(beside, ((0, 0), (0, wider)))], axis=0)

    def parted(got):
        vector = got[-depth:].astype(F32)
        return got[:-depth], sum(
            vector[:, k * 2 * LANES : (k + 1) * 2 * LANES] for k in range(3))

    if n_y == 2:
        got, more = parted(swap(joined(pick(parts, 1 - i_y), sums), "y"))
        parts, sums = pick(parts, i_y) + got, sums + more
    else:
        parts = lax.psum_scatter(parts, "y", scatter_dimension=0, tiled=False)
        sums = lax.psum(sums, "y")
    up.advance()
    grad_tokens = last(
        ids, dh_own, after(swap(dh_other, "c"), parts, up.sent), tokens, dy, a_gain)

    owners = []
    for y in range(n_y):
        for x in range(2):
            for z in range(n_z):
                for c in range(2):
                    source = ((y * 2 + x) * n_z + z) * 2 + c
                    owners.append((source, n_y * n_z * (2 * x + c) + z * n_y + y))
    share_down = lax.ppermute(after(down.finish(), *late), ALL, owners)
    share_down = after(share_down, grad_tokens, up.sent).astype(F32)

    def spread(parts):
        got = swap(pick(parts, 1 - i_c, 1), "c")
        cols = in_order(i_c, pick(parts, i_c, 1), got, 2)
        got = swap(pick(cols, 1 - i_x), "x")
        return in_order(i_x, pick(cols, i_x), got, 1).astype(F32)

    share_gate = spread(gate.finish(grad_tokens))
    share_up = spread(up.finish())

    parts = parts.reshape(n_z, 2 * row_block, half + 2 * LANES)
    kept_z, sums_z = pick(parts, i_z), sums
    out_sum, by_step = kept_z[:, :half].astype(F32), [kept_z[:, half:]]
    for s in steps:
        got, more = parted(crossed(joined(pick(parts, i_z ^ s), sums), s, n_z))
        out_sum, sums_z = out_sum + got[:, :half].astype(F32), sums_z + more
        by_step.append(got[:, half:])
    merged = jnp.concatenate([out_sum.astype(BF16), *by_step], axis=1)
    merged = merged.reshape(2, row_block, merged.shape[1])
    got, more = parted(swap(joined(pick(merged, 1 - i_c), sums_z), "c"))
    sums = (sums_z + more).reshape(-1)
    share_out, share_query, share_key, share_value = unpack(ids, pick(merged, i_c), got, half)

    return (
        mixed,
        grad_tokens,
        sums[:width],
        share_query,
        share_key,
        share_value,
        sums[2 * width : 2 * width + head_size],
        sums[2 * width + head_size : total],
        share_out,
        sums[width : 2 * width],
        share_gate,
        share_up,
        share_down,
    )


def solution(mesh):
    n_dp, n_seq = mesh.shape["dp"], mesh.shape["seq"]
    fine = Mesh(mesh.devices.reshape(n_dp // 2, 2, n_seq // 2, 2), ALL)
    split = P(ALL, None)
    in_specs = (split, P(("y", "x"), None)) + (P(),) * 11 + (split,)
    out_specs = (split, split, P(), split, split, split, P(), P(), split, P(), split, split, split)
    return jax.shard_map(body, mesh=fine, in_specs=in_specs, out_specs=out_specs, check_vma=False)
```
